512 devices in a mesh: dp: 16 (over y, x), ctx: 16 (over z), tp: 2 (over core).
Axes of the slice: x: 4, y: 4, z: 16, core: 2. Of those that a mesh axis runs over, the one named last changes fastest.
Arguments:
- q_proj: bfloat16 [16, 2048, 4096], P('dp', 'ctx', 'tp'), may hold values from -6 to 6
- q_bias: bfloat16 [4096], P('tp'), may hold values from -3 to 3
- k_proj: bfloat16 [16, 2048, 512], P('dp', 'ctx', 'tp'), may hold values from -6 to 6
- v_proj: bfloat16 [16, 2048, 512], P('dp', 'ctx', 'tp'), may hold values from -6 to 6
- v_bias: bfloat16 [512], P('tp'), may hold values from -3 to 3
- dout: bfloat16 [16, 2048, 4096], P('dp', 'ctx', 'tp'), may hold values from -6 to 6
- lengths: int32 [16, 8], P('dp'), may hold values from 1 to 1536, 2048 in all within a row
Outputs:
- attn_out: bfloat16 [16, 2048, 4096], P('dp', 'ctx', 'tp')
- q_grad: bfloat16 [16, 2048, 4096], P('dp', 'ctx', 'tp')
- k_grad: bfloat16 [16, 2048, 512], P('dp', 'ctx', 'tp')
- v_grad: bfloat16 [16, 2048, 512], P('dp', 'ctx', 'tp')
- q_bias_grad: float32 [4096], P('tp')
- v_bias_grad: float32 [512], P('tp')
The draws below stay inside these ranges and needn't reach their ends.
All inputs are finite; a program needn't handle non-finite values.
Results may differ from the reference program's by a relative error of at most 0.035.
Values may be sent and summed in bfloat16 or wider, within the bound.
A program may use at most 64 MiB of HBM per device.

```python
import math
import jax
import jax.numpy as jnp
import numpy as np
from jax import lax

HEAD_DIM = 128
HEADS = 32
KV_HEADS = 4
DOCS = 8
TOKENS = 2048
BATCH = 16
MOST = 1536


def draw_q_proj(key, part):
    key = jax.random.fold_in(key, 1)
    shape = (BATCH, TOKENS, KV_HEADS, HEADS // KV_HEADS, HEAD_DIM)
    base = jnp.clip(1.5 * jax.random.normal(key, shape, jnp.float32), -6.0, 6.0)
    return base.reshape(BATCH, TOKENS, HEADS * HEAD_DIM).astype(jnp.bfloat16)


def draw_k_proj(key, part):
    key = jax.random.fold_in(key, 2)
    shape = (BATCH, TOKENS, KV_HEADS, HEAD_DIM)
    base = jnp.clip(1.3 * jax.random.normal(key, shape, jnp.float32), -6.0, 6.0)
    return base.reshape(BATCH, TOKENS, KV_HEADS * HEAD_DIM).astype(jnp.bfloat16)


def block_scale(key, extent, split, least, high):
    loudness = 1.0
    for axis_at, parts in split:
        steps = jax.random.uniform(jax.random.fold_in(jax.random.fold_in(key, 6), axis_at), (parts,), jnp.float32, least / len(split), high / len(split))
        loudness = loudness * jnp.repeat(jnp.exp(steps), extent[axis_at] // parts).reshape((-1,) + (1,) * (len(extent) - 1 - axis_at))
    return loudness


def length_profile(count, total, reach, skew):
    portions = [(1 << 20) // math.isqrt(grade ** skew) + 1 for grade in range(2, count + 1)]
    surplus, holding = total - reach - (count - 1), [1] * (count - 1)
    while surplus > 0:
        free = [i for i in range(count - 1) if holding[i] < reach]
        pool, remaining = sum([portions[i] for i in free]), surplus
        for i in free:
            more = min(reach - holding[i], max(1, remaining * portions[i] // pool), surplus)
            holding[i] = holding[i] + more
            surplus = surplus - more
    return np.array([reach] + holding)


def uneven_parts(own_key, number_of, total, bound, skew):
    if number_of == 2:
        one = jax.random.randint(own_key, (), max(1, total - bound), min(bound, total - 1) + 1)
        return jnp.stack([one, total - one])
    sizes = jnp.asarray(length_profile(number_of, total, bound, skew), jnp.int32)
    couples = (number_of - 1) // 2
    donor, receiver = sizes[1:1 + 2 * couples:2], sizes[2:2 + 2 * couples:2]
    margin = jnp.minimum(donor - 1, bound - receiver)
    shifted = jax.random.randint(jax.random.fold_in(own_key, 1), (couples,), 0, 1 << 20) % (margin + 1)
    sizes = sizes.at[1:1 + 2 * couples:2].set(donor - shifted).at[2:2 + 2 * couples:2].set(receiver + shifted)
    return sizes[jax.random.permutation(jax.random.fold_in(own_key, 2), number_of)]


def noise(rng, shape, deviation, most, shards=(), held_as=jnp.bfloat16):
    level = block_scale(rng, shape, shards, -0.22, 0.18) if shards else 1.0
    entries = jax.random.normal(rng, shape, jnp.float32) * deviation * level
    return jnp.minimum(jnp.maximum(entries, -most), most).astype(held_as)


def setup_inputs(seed: int = 0) -> dict:
    streams_of = jax.random.split(jax.random.key(seed), 8)
    q_proj = draw_q_proj(jax.random.fold_in(streams_of[7], 71), 0)
    q_bias = noise(streams_of[1], (HEADS * HEAD_DIM,), 0.5, 3.0, ((0, 2),))
    k_proj = draw_k_proj(jax.random.fold_in(streams_of[7], 71), 0)
    v_proj = noise(streams_of[3], (BATCH, TOKENS, KV_HEADS * HEAD_DIM), 1.0, 6.0, ((0, 16), (1, 16), (2, 2)))
    v_bias = noise(streams_of[4], (KV_HEADS * HEAD_DIM,), 0.5, 3.0, ((0, 2),))
    dout = noise(streams_of[5], (BATCH, TOKENS, HEADS * HEAD_DIM), 1.0, 6.0, ((0, 16), (1, 16), (2, 2)))
    lengths = jax.vmap(lambda own: uneven_parts(own, DOCS, TOKENS, MOST, 2))(jax.random.split(streams_of[6], BATCH)).reshape((BATCH, DOCS)).astype(jnp.int32)
    return dict(q_proj=q_proj, q_bias=q_bias, k_proj=k_proj, v_proj=v_proj, v_bias=v_bias, dout=dout, lengths=lengths)


def doc_index(lengths_row, positions):
    ends = jnp.cumsum(lengths_row).astype(jnp.int32)
    return jnp.sum((positions[:, None] >= ends[None, :]).astype(jnp.int32), axis=1)


def round_keep(array):
    return lax.optimization_barrier(array.astype(jnp.bfloat16)).astype(jnp.float32)


def head_group(queries, keys, values, grads, live):
    scale = HEAD_DIM ** -0.5
    score = jnp.einsum('gtd,sd->gts', queries, keys) * scale
    mask = live[None]
    row_max = jnp.max(jnp.where(mask, score, -1e30), axis=-1)
    weights = jnp.where(mask, jnp.exp(score - row_max[..., None]), 0.0)
    total = jnp.sum(weights, axis=-1)
    weights_b = round_keep(weights)
    attn = (jnp.einsum('gts,sd->gtd', weights_b, values) / total[..., None]).astype(jnp.bfloat16)
    lse = row_max + jnp.log(total)
    delta = jnp.sum(grads * attn.astype(jnp.float32), axis=-1)
    probs = jnp.where(mask, jnp.exp(score - lse[..., None]), 0.0)
    probs_b = round_keep(probs)
    value_grad = jnp.einsum('gts,gtd->sd', probs_b, grads)
    dprob = jnp.einsum('gtd,sd->gts', grads, values)
    dscore = round_keep(probs * (dprob - delta[..., None]))
    query_grad = jnp.einsum('gts,sd->gtd', dscore, keys) * scale
    key_grad = jnp.einsum('gts,gtd->sd', dscore, queries) * scale
    return attn, query_grad, key_grad, value_grad


def reference(q_proj, q_bias, k_proj, v_proj, v_bias, dout, lengths):
    group = HEADS // KV_HEADS
    positions = jnp.arange(TOKENS, dtype=jnp.int32)

    def one_batch(items):
        q_part, k_part, v_part, g_part, lens = items
        queries = round_keep(q_part.astype(jnp.float32) + q_bias.astype(jnp.float32))
        values = round_keep(v_part.astype(jnp.float32) + v_bias.astype(jnp.float32))
        keys = k_part.astype(jnp.float32)
        doc = doc_index(lens, positions)
        live = (positions[None, :] <= positions[:, None]) & (doc[None, :] == doc[:, None])
        q_heads = queries.reshape(TOKENS, KV_HEADS, group, HEAD_DIM)
        g_heads = g_part.astype(jnp.float32).reshape(TOKENS, KV_HEADS, group, HEAD_DIM)
        attn_list, qg_list, kg_list, vg_list = [], [], [], []
        for head in range(KV_HEADS):
            cols = slice(head * HEAD_DIM, (head + 1) * HEAD_DIM)
            attn, qg, kg, vg = head_group(q_heads[:, head].transpose(1, 0, 2), keys[:, cols], values[:, cols], g_heads[:, head].transpose(1, 0, 2), live)
            attn_list.append(attn.transpose(1, 0, 2))
            qg_list.append(qg.transpose(1, 0, 2))
            kg_list.append(kg)
            vg_list.append(vg)
        attn_all = jnp.stack(attn_list, axis=1).reshape(TOKENS, HEADS * HEAD_DIM)
        qg_all = jnp.stack(qg_list, axis=1).reshape(TOKENS, HEADS * HEAD_DIM)
        kg_all = jnp.concatenate(kg_list, axis=1)
        vg_all = jnp.concatenate(vg_list, axis=1)
        return (attn_all, qg_all.astype(jnp.bfloat16), kg_all.astype(jnp.bfloat16), vg_all.astype(jnp.bfloat16), jnp.sum(qg_all, axis=0), jnp.sum(vg_all, axis=0))

    attn_out, q_grad, k_grad, v_grad, q_sums, v_sums = lax.map(one_batch, (q_proj, k_proj, v_proj, dout, lengths))
    q_bias_grad = jnp.sum(q_sums, axis=0) / BATCH
    v_bias_grad = jnp.sum(v_sums, axis=0) / BATCH
    return (attn_out, q_grad, k_grad, v_grad, q_bias_grad, v_bias_grad)
```

```python
import math

import jax
import jax.numpy as jnp
from jax import lax
from jax.experimental import pallas as pl
from jax.experimental.pallas import tpu as pltpu
from jax.sharding import PartitionSpec as P

HEAD_DIM = 128
SCALE = HEAD_DIM ** -0.5
LOG2E = math.log2(math.e)
NEG = -1e30
BLOCK = 128
KV = 2
GROUP = 8
TILES = 4
RING = 16
CHUNKS = 7
F32 = jnp.float32
BF16 = jnp.bfloat16


def slot_left(k):
    return k + 1 + ((k + 11) // 16) * (k - 5)


def slot_right(k):
    return 17 - k + ((k + 12) // 16) * (3 * k - 18)


def nearest(c):
    far = (c + 13) // 16
    return (2 * c - 1) * (1 - far) + (c + 2) * far


def kernel(
    q_hbm, qb_ref, k_hbm, v_hbm, vb_ref, g_hbm, len_ref,
    attn_hbm, qg_hbm, kg_ref, vg_ref, qbg_ref, vbg_ref,
    q_in, k_in, v_in, g_in, q_rows, g_rows, q_cols, g_cols, kv, scores, top, total, delta, acc, q_acc, terms,
    attn_out, qg_out, v_sum,
    left_in, right_in, left_out, right_out, share, share_z, part, share_d, final,
    load_sem, store_sem, ag_send, ag_recv, rs_send, rs_recv, ar_send, ar_recv,
):
    dp, me, tp = lax.axis_index("dp"), lax.axis_index("ctx"), lax.axis_index("tp")
    dps = lax.axis_size("dp")
    right, left = lax.rem(me + 1, RING), lax.rem(me + RING - 1, RING)
    to_right, to_left = (dp, right, tp), (dp, left, tp)

    def z_peer(o):
        return lax.rem(me + o, RING)

    def d_peer(o):
        return lax.rem(dp + o, dps)

    loads = [
        pltpu.make_async_copy(src, dst, load_sem.at[i])
        for i, (src, dst) in enumerate(((k_hbm, k_in), (v_hbm, v_in), (q_hbm, q_in), (g_hbm, g_in)))
    ]
    for copy in loads:
        copy.start()

    barrier = pltpu.get_barrier_semaphore()

    def greet_z(o, _):
        pl.semaphore_signal(barrier, inc=1, device_id=(dp, z_peer(o), tp), device_id_type=pl.DeviceIdType.MESH)
        return 0

    def greet_d(o, _):
        pl.semaphore_signal(barrier, inc=1, device_id=(d_peer(o), me, tp), device_id_type=pl.DeviceIdType.MESH)
        return 0

    lax.fori_loop(1, RING, greet_z, 0)
    lax.fori_loop(1, dps, greet_d, 0)

    def remote(src, dst, send, recv, device):
        return pltpu.make_async_remote_copy(
            src_ref=src, dst_ref=dst, send_sem=send, recv_sem=recv, device_id=device, device_id_type=pl.DeviceIdType.MESH
        )

    def ag(way, src, dst, k, h):
        return remote(kv.at[src, h], kv.at[dst, h], ag_send.at[way, k, h], ag_recv.at[way, k, h], (to_right, to_left)[way])

    loads[0].wait()
    loads[1].wait()
    values = (v_in[...].astype(F32) + vb_ref[...].astype(F32)).astype(BF16)
    for h in range(KV):
        kv[0, h, 0] = k_in[:, h * 128:(h + 1) * 128]
        kv[0, h, 1] = values[:, h * 128:(h + 1) * 128]
    kv[1] = jnp.zeros((KV, 2, BLOCK, HEAD_DIM), BF16)
    pl.semaphore_wait(barrier, RING - 1 + dps - 1)
    for h in range(KV):
        ag(0, 0, slot_left(1), 1, h).start()
        ag(1, 0, slot_right(1), 1, h).start()

    loads[2].wait()
    loads[3].wait()
    for h in range(KV):
        for j in range(TILES):
            for e in range(2):
                at = (h * GROUP + j * 2 + e) * 128
                rows = slice(e * 128, (e + 1) * 128)
                block = (q_in[:, at:at + 128].astype(F32) + qb_ref[:, at:at + 128].astype(F32)).astype(BF16)
                q_rows[h, j, rows, :] = block
                q_cols[h, j, :, rows] = block.T
                block = g_in[:, at:at + 128]
                g_rows[h, j, rows, :] = block
                g_cols[h, j, :, rows] = block.T
    top[...] = jnp.full(top.shape, NEG, F32)
    total[...] = jnp.zeros(total.shape, F32)
    acc[...] = jnp.zeros(acc.shape, F32)
    q_acc[...] = jnp.zeros(q_acc.shape, F32)
    v_sum[...] = jnp.zeros(v_sum.shape, F32)
    share[...] = jnp.zeros(share.shape, F32)

    position = me * BLOCK + lax.broadcasted_iota(jnp.int32, (1, BLOCK), 1)
    begin = jnp.zeros((1, BLOCK), jnp.int32)
    end = jnp.int32(0)
    for d in range(len_ref.shape[1]):
        end = end + len_ref[0, d]
        begin = jnp.where(position >= end, end, begin)

    def forward(c, h):
        near = nearest(c)
        far = jnp.where(c == 0, -1, jnp.where(c <= 2, 2 * c, 15 - c))
        offset = lax.broadcasted_iota(jnp.int32, (BLOCK, BLOCK), 0)
        bias = []
        for d in (jnp.where(c == 0, 0, near), far):
            at = (me - d) * BLOCK + offset
            bias.append(jnp.where((at >= begin) & (at <= position), 0.0, NEG).astype(F32))
        bias = jnp.concatenate(bias, axis=0)
        bias = jnp.concatenate([bias, bias], axis=1)
        pair = kv[pl.ds(2 * c, 2), h]
        keys = pair[:, 0].reshape(2 * BLOCK, HEAD_DIM)
        values_t = pair[:, 1].reshape(2 * BLOCK, HEAD_DIM).T
        for j in range(TILES):
            score = jnp.dot(keys, q_cols[h, j], preferred_element_type=F32) * (SCALE * LOG2E) + bias
            scores[c, h, j] = score
            old = top[h, j]
            new = jnp.maximum(old, jnp.max(score, axis=0, keepdims=True))
            fade = jnp.exp2(old - new)
            weights = jnp.exp2(score - new)
            top[h, j] = new
            total[h, j] = total[h, j] * fade + jnp.sum(weights, axis=0, keepdims=True)
            acc[h, j] = acc[h, j] * fade + jnp.dot(values_t, weights.astype(BF16), preferred_element_type=F32)

    def pass_on(k, h):
        @pl.when((k < 8) | (h == 0))
        def _():
            here = slot_left(k)
            ag(0, here, here, k, h).wait_recv()

            @pl.when((k < 7) | ((k == 7) & (h == 0)))
            def _():
                ag(0, here, slot_left(k + 1), k + 1, h).start()

        @pl.when(k < 8)
        def _():
            here = slot_right(k)
            ag(1, here, here, k, h).wait_recv()

            @pl.when(k < 7)
            def _():
                ag(1, here, slot_right(k + 1), k + 1, h).start()

            @pl.when((k == 7) & (h == 1))
            def _():
                ag(1, here, 12, 8, h).start()

        @pl.when((k == 8) & (h == 1))
        def _():
            ag(1, 12, 12, 8, h).wait_recv()

    def forward_step(i, _):
        c, h = i // 2, i % 2

        @pl.when((c >= 1) & (c <= 2))
        def _():
            @pl.when(h == 0)
            def _():
                pass_on(2 * c - 1, 0)
                pass_on(2 * c - 1, 1)

            pass_on(2 * c, h)

        @pl.when(c >= 3)
        def _():
            pass_on(c + 2, h)

        live = me >= nearest(c)

        @pl.when(live)
        def _():
            forward(c, h)

        @pl.when(jnp.logical_not(live))
        def _():
            terms[pl.ds(2 * c, 2), h] = jnp.zeros((2, 2, BLOCK, HEAD_DIM), F32)

        return 0

    lax.fori_loop(0, CHUNKS * KV, forward_step, 0)

    for h in range(KV):
        for j in range(TILES):
            amount = total[h, j]
            out = (acc[h, j] * (1.0 / amount)).astype(BF16)
            delta[h, j] = jnp.sum(out.astype(F32) * g_cols[h, j].astype(F32), axis=0, keepdims=True)
            top[h, j] = top[h, j] + jnp.log2(amount)
            for e in range(2):
                at = (h * GROUP + j * 2 + e) * 128
                attn_out[:, at:at + 128] = out[:, e * 128:(e + 1) * 128].T
    store_attn = pltpu.make_async_copy(attn_out, attn_hbm, store_sem.at[0])
    store_attn.start()

    def backward(c, h):
        pair = kv[pl.ds(2 * c, 2), h]
        keys_t = pair[:, 0].reshape(2 * BLOCK, HEAD_DIM).T
        values = pair[:, 1].reshape(2 * BLOCK, HEAD_DIM)
        v_term = jnp.zeros((2 * BLOCK, HEAD_DIM), F32)
        k_term = jnp.zeros((2 * BLOCK, HEAD_DIM), F32)
        for j in range(TILES):
            probs = jnp.exp2(scores[c, h, j] - top[h, j])
            dprob = jnp.dot(values, g_cols[h, j], preferred_element_type=F32)
            dscore = (probs * (dprob - delta[h, j])).astype(BF16)
            v_term += jnp.dot(probs.astype(BF16), g_rows[h, j], preferred_element_type=F32)
            k_term += jnp.dot(dscore, q_rows[h, j], preferred_element_type=F32)
            q_acc[h, j] += jnp.dot(keys_t, dscore, preferred_element_type=F32)
        terms[pl.ds(2 * c, 2), h, 0] = (k_term * SCALE).reshape(2, BLOCK, HEAD_DIM)
        terms[pl.ds(2 * c, 2), h, 1] = v_term.reshape(2, BLOCK, HEAD_DIM)
        v_sum[h] += jnp.sum(v_term, axis=0, keepdims=True)

    def rs(way, src, k, h):
        return remote(src, (left_in, right_in)[way].at[k - 1, h], rs_send.at[way, k, h], rs_recv.at[way, k - 1, h], (to_left, to_right)[way])

    def arrived(way, k, h):
        into = (left_in, right_in)[way].at[k, h]
        remote(into, into, rs_send.at[way, k, h], rs_recv.at[way, k, h], (to_left, to_right)[way]).wait_recv()

    def begin_sum(way, k, h, slot):
        held = (left_out, right_out)[way]
        held[k, h] = terms[slot, h].astype(BF16)
        rs(way, held.at[k, h], k, h).start()

    def add_sum(way, k, h, slot):
        arrived(way, k, h)
        held = (left_out, right_out)[way]
        held[k, h] = (terms[slot, h] + (left_in, right_in)[way][k, h].astype(F32)).astype(BF16)
        rs(way, held.at[k, h], k, h).start()

    def backward_step(i, h):
        c = CHUNKS - 1 - i

        @pl.when(me >= nearest(c))
        def _():
            backward(c, h)

        k = 8 - i

        @pl.when(((i == 0) & (h == 0)) | ((i == 1) & (h == 1)))
        def _():
            begin_sum(0, k, h, slot_left(k))

        @pl.when((i >= 2) | ((i == 1) & (h == 0)))
        def _():
            add_sum(0, k, h, slot_left(k))

        k2 = 7 - i

        @pl.when((i == 0) & (h == 0))
        def _():
            begin_sum(1, k2, h, slot_right(k2))

        @pl.when((i == 0) & (h == 1))
        def _():
            begin_sum(1, 8, h, 12)

        @pl.when(((i >= 1) & (i <= 3)) | ((i == 0) & (h == 1)))
        def _():
            add_sum(1, k2, h, slot_right(k2))

        @pl.when((i >= 4) & (i <= 6))
        def _():
            arrived(1, k2, h)
            rs(1, right_in.at[k2, h], k2, h).start()

    def backward_loop(n, _):
        backward_step(n // 2, n % 2)
        return 0

    lax.fori_loop(0, CHUNKS * KV, backward_loop, 0)

    for h in range(KV):
        for j in range(TILES):
            for e in range(2):
                head = h * GROUP + j * 2 + e
                grad = q_acc[h, j, :, e * 128:(e + 1) * 128].T * SCALE
                share[head, 0:1, :] = jnp.sum(grad, axis=0, keepdims=True)
                qg_out[:, head * 128:(head + 1) * 128] = grad.astype(BF16)
        share[h, 1:2, :] = v_sum[h]
    store_qg = pltpu.make_async_copy(qg_out, qg_hbm, store_sem.at[1])
    store_qg.start()

    def ar_z(o):
        return remote(share.at[z_peer(o)], share_z.at[o], ar_send.at[0, o], ar_recv.at[0, o], (dp, z_peer(o), tp))

    def ar_d(o):
        return remote(part, share_d.at[o], ar_send.at[1, o], ar_recv.at[1, o], (d_peer(o), me, tp))

    def ar_back(o):
        return remote(final.at[me], final.at[me], ar_send.at[2, o], ar_recv.at[2, o], (dp, z_peer(o), tp))

    def ar_back_in(o):
        source = lax.rem(me + RING - o, RING)
        return remote(final.at[source], final.at[source], ar_send.at[2, o], ar_recv.at[2, o], (dp, z_peer(o), tp))

    def each(last, act):
        def body(o, _):
            act(o)
            return 0

        lax.fori_loop(1, last, body, 0)

    each(RING, lambda o: ar_z(o).start())
    for h in range(KV):
        add_sum(0, 1, h, slot_left(1))

    each(RING, lambda o: ar_z(o).wait_recv())
    share_z[0] = share[me]
    part[...] = jnp.sum(share_z[...], axis=0)
    each(dps, lambda o: ar_d(o).start())
    each(dps, lambda o: ar_d(o).wait_recv())
    share_d[0] = part[...]
    final[me] = jnp.sum(share_d[...], axis=0) * (1.0 / dps)
    each(RING, lambda o: ar_back(o).start())

    for h in range(KV):
        arrived(0, 0, h)
        arrived(1, 0, h)
        both = terms[0, h] + left_in[0, h].astype(F32) + right_in[0, h].astype(F32)
        kg_ref[:, h * 128:(h + 1) * 128] = both[0].astype(BF16)
        vg_ref[:, h * 128:(h + 1) * 128] = both[1].astype(BF16)

    each(RING, lambda o: ar_back_in(o).wait_recv())
    for p in range(RING):
        qbg_ref[p:p + 1, :] = final[p, 0:1, :]
    for h in range(KV):
        vbg_ref[h:h + 1, :] = final[h, 1:2, :]

    def sent(n, _):
        k, h = n // 2 + 1, n % 2
        ag(0, 0, 0, k, h).wait_send()
        ag(1, 0, 0, k, h).wait_send()
        rs(0, left_out.at[k, h], k, h).wait_send()
        rs(1, right_out.at[k, h], k, h).wait_send()
        return 0

    lax.fori_loop(0, 14, sent, 0)
    ag(0, 0, 0, 8, 0).wait_send()
    ag(1, 0, 0, 8, 1).wait_send()
    rs(0, left_out.at[8, 0], 8, 0).wait_send()
    rs(1, right_out.at[8, 1], 8, 1).wait_send()
    each(RING, lambda o: ar_z(o).wait_send())
    each(dps, lambda o: ar_d(o).wait_send())
    each(RING, lambda o: ar_back(o).wait_send())
    store_attn.wait()
    store_qg.wait()


def shards(q_proj, q_bias, k_proj, v_proj, v_bias, dout, lengths):
    width, kv_width = q_proj.shape[2], k_proj.shape[2]
    dps = lax.axis_size("dp")
    any_space = pl.BlockSpec(memory_space=pl.ANY)
    vmem = pl.BlockSpec(memory_space=pltpu.VMEM)
    block = (KV, 2, BLOCK, HEAD_DIM)
    attn, q_grad, k_grad, v_grad, q_sums, v_sums = pl.pallas_call(
        kernel,
        out_shape=(
            jax.ShapeDtypeStruct((BLOCK, width), BF16),
            jax.ShapeDtypeStruct((BLOCK, width), BF16),
            jax.ShapeDtypeStruct((BLOCK, kv_width), BF16),
            jax.ShapeDtypeStruct((BLOCK, kv_width), BF16),
            jax.ShapeDtypeStruct((KV * GROUP, HEAD_DIM), F32),
            jax.ShapeDtypeStruct((KV, HEAD_DIM), F32),
        ),
        in_specs=[any_space, vmem, any_space, any_space, vmem, any_space, pl.BlockSpec(memory_space=pltpu.SMEM)],
        out_specs=(any_space, any_space, vmem, vmem, vmem, vmem),
        scratch_shapes=[
            pltpu.VMEM((BLOCK, width), BF16),
            pltpu.VMEM((BLOCK, kv_width), BF16),
            pltpu.VMEM((BLOCK, kv_width), BF16),
            pltpu.VMEM((BLOCK, width), BF16),
            pltpu.VMEM((KV, TILES, 2 * BLOCK, HEAD_DIM), BF16),
            pltpu.VMEM((KV, TILES, 2 * BLOCK, HEAD_DIM), BF16),
            pltpu.VMEM((KV, TILES, HEAD_DIM, 2 * BLOCK), BF16),
            pltpu.VMEM((KV, TILES, HEAD_DIM, 2 * BLOCK), BF16),
            pltpu.VMEM((17,) + block, BF16),
            pltpu.VMEM((CHUNKS, KV, TILES, 2 * BLOCK, 2 * BLOCK), F32),
            pltpu.VMEM((KV, TILES, 1, 2 * BLOCK), F32),
            pltpu.VMEM((KV, TILES, 1, 2 * BLOCK), F32),
            pltpu.VMEM((KV, TILES, 1, 2 * BLOCK), F32),
            pltpu.VMEM((KV, TILES, HEAD_DIM, 2 * BLOCK), F32),
            pltpu.VMEM((KV, TILES, HEAD_DIM, 2 * BLOCK), F32),
            pltpu.VMEM((2 * CHUNKS,) + block, F32),
            pltpu.VMEM((BLOCK, width), BF16),
            pltpu.VMEM((BLOCK, width), BF16),
            pltpu.VMEM((KV, 1, HEAD_DIM), F32),
            pltpu.VMEM((8,) + block, BF16),
            pltpu.VMEM((8,) + block, BF16),
            pltpu.VMEM((9,) + block, BF16),
            pltpu.VMEM((9,) + block, BF16),
            pltpu.VMEM((RING, 8, HEAD_DIM), F32),
            pltpu.VMEM((RING, 8, HEAD_DIM), F32),
            pltpu.VMEM((8, HEAD_DIM), F32),
            pltpu.VMEM((dps, 8, HEAD_DIM), F32),
            pltpu.VMEM((RING, 8, HEAD_DIM), F32),
            pltpu.SemaphoreType.DMA((4,)),
            pltpu.SemaphoreType.DMA((2,)),
            pltpu.SemaphoreType.DMA((2, 9, KV)),
            pltpu.SemaphoreType.DMA((2, 9, KV)),
            pltpu.SemaphoreType.DMA((2, 9, KV)),
            pltpu.SemaphoreType.DMA((2, 9, KV)),
            pltpu.SemaphoreType.DMA((3, RING)),
            pltpu.SemaphoreType.DMA((3, RING)),
        ],
        compiler_params=pltpu.CompilerParams(
            collective_id=0, has_side_effects=True, vmem_limit_bytes=48 * 2**20
        ),
        cost_estimate=pl.CostEstimate(flops=6 * 10**9, bytes_accessed=3 * 10**6, transcendentals=7 * 10**6),
    )(
        q_proj[0],
        q_bias.reshape(1, -1),
        k_proj[0],
        v_proj[0],
        v_bias.reshape(1, -1),
        dout[0],
        lengths,
    )
    return attn[None], q_grad[None], k_grad[None], v_grad[None], q_sums.reshape(-1), v_sums.reshape(-1)


def solution(mesh):
    placed = (
        P("dp", "ctx", "tp"),
        P("tp"),
        P("dp", "ctx", "tp"),
        P("dp", "ctx", "tp"),
        P("tp"),
        P("dp", "ctx", "tp"),
        P("dp", None),
    )
    return jax.shard_map(
        shards,
        mesh=mesh,
        in_specs=placed,
        out_specs=(
            P("dp", "ctx", "tp"),
            P("dp", "ctx", "tp"),
            P("dp", "ctx", "tp"),
            P("dp", "ctx", "tp"),
            P("tp"),
            P("tp"),
        ),
        check_vma=False,
    )
```

```python
import math

import jax
import jax.numpy as jnp
from jax import lax
from jax.experimental import pallas as pl
from jax.experimental.pallas import tpu as pltpu
from jax.sharding import PartitionSpec as P

HEAD_DIM = 128
SCALE = HEAD_DIM ** -0.5
LOG2E = math.log2(math.e)
NEG = -1e30
BLOCK = 128
KV = 2
GROUP = 8
TILES = 4
RING = 16
CHUNKS = 7
F32 = jnp.float32
BF16 = jnp.bfloat16

PAIRS = ((0, None), (3, 12), (1, 2), (4, 11), (5, 10), (6, 9), (7, 8))
SLOT = {d: 2 * c + n for c, pair in enumerate(PAIRS) for n, d in enumerate(pair) if d is not None}
NEXT = {1: 2, 3: 4, 4: 5, 5: 6, 6: 7, 12: 11, 11: 10, 10: 9, 9: 8}
FIRST = (12, 3, 1)
SUMS = {7: (6, -1), 6: (5, -1), 5: (4, -1), 4: (3, -1), 3: (2, -3), 2: (1, -1), 1: (0, -1),
        8: (9, 1), 9: (10, 1), 10: (11, 1), 11: (12, 1), 12: (7, 4)}
ROWS = 24


def nearest(c):
    return 3 * ((c + 6) // 7) - 2 * ((c + 5) // 7) + c * ((c + 4) // 7)


def kernel(
    q_hbm, qb_hbm, k_hbm, v_hbm, vb_hbm, g_hbm, len_hbm,
    attn_hbm, qg_hbm, kg_hbm, vg_hbm, qbg_hbm, vbg_hbm,
    attn_out, qg_out, kg_ref, vg_ref, qbg_ref, vbg_ref, q_in, qb_in, k_in, v_in, vb_in, g_in, lens, q_rows, g_rows, q_cols, g_cols, kv, scores, top, total, delta, acc, q_acc, terms,
    v_sum, sum_in, sum_out, share, share_d, part, share_z,
    load_sem, store_sem, ag_send, ag_recv, rs_send, rs_recv, ar_send, ar_recv,
):
    dp, me, tp = lax.axis_index("dp"), lax.axis_index("ctx"), lax.axis_index("tp")
    dps = lax.axis_size("dp")

    def z_peer(o):
        return lax.rem(me + RING + o, RING)

    def d_peer(o):
        return lax.rem(dp + o, dps)

    loads = [
        pltpu.make_async_copy(src, dst, load_sem.at[i])
        for i, (src, dst) in enumerate((
            (k_hbm, k_in), (v_hbm, v_in), (vb_hbm, vb_in), (q_hbm, q_in), (g_hbm, g_in), (qb_hbm, qb_in), (len_hbm, lens)))
    ]
    for copy in loads:
        copy.start()

    stores = [
        pltpu.make_async_copy(src, dst, store_sem.at[i])
        for i, (src, dst) in enumerate((
            (attn_out, attn_hbm), (qg_out, qg_hbm), (kg_ref, kg_hbm), (vg_ref, vg_hbm), (qbg_ref, qbg_hbm), (vbg_ref, vbg_hbm)))
    ]
    barrier = pltpu.get_barrier_semaphore()

    def greet_z(o, _):
        pl.semaphore_signal(barrier, inc=1, device_id=(dp, z_peer(o), tp), device_id_type=pl.DeviceIdType.MESH)
        return 0

    def greet_d(o, _):
        pl.semaphore_signal(barrier, inc=1, device_id=(d_peer(o), me, tp), device_id_type=pl.DeviceIdType.MESH)
        return 0

    lax.fori_loop(1, RING, greet_z, 0)
    lax.fori_loop(1, dps, greet_d, 0)

    def remote(src, dst, send, recv, device):
        return pltpu.make_async_remote_copy(
            src_ref=src, dst_ref=dst, send_sem=send, recv_sem=recv, device_id=device, device_id_type=pl.DeviceIdType.MESH
        )

    def held(d):
        return me >= d if d <= 7 else lax.rem(me + RING - d, RING) <= 7

    def ag(d, to, h, n):
        step = to - d if to <= 7 else (-4 if d == 0 else -1)
        return remote(kv.at[SLOT[d], h, n], kv.at[SLOT[to], h, n], ag_send.at[to, h, n], ag_recv.at[to, h, n], (dp, z_peer(step), tp))

    def sends(d, to):
        return (held(d) & (me + to - d < RING)) if to <= 7 else held(d)

    for copy in loads[:3]:
        copy.wait()
    for h in range(KV):
        cols = slice(h * 128, (h + 1) * 128)
        kv[0, h, 0] = k_in[:, cols]
        kv[0, h, 1] = (v_in[:, cols].astype(F32) + vb_in[h:h + 1, :].astype(F32)).astype(BF16)
    nothing = jnp.zeros((KV, 2, BLOCK, HEAD_DIM), BF16)
    kv[1] = nothing
    pl.semaphore_wait(barrier, RING - 1 + dps - 1)
    for to in FIRST:
        @pl.when(me <= 7 if to == 12 else me + to < RING)
        def _(to=to):
            for h in range(KV):
                for n in range(2):
                    ag(0, to, h, n).start()

    for d in (2, 8, 9, 10, 11, 12):
        @pl.when(jnp.logical_not(held(d)))
        def _(d=d):
            kv[SLOT[d]] = nothing

    for copy in loads[3:]:
        copy.wait()
    for h in range(KV):
        for j in range(TILES):
            for e in range(2):
                head = h * GROUP + j * 2 + e
                cols = slice(head * 128, (head + 1) * 128)
                rows = slice(e * 128, (e + 1) * 128)
                block = (q_in[:, cols].astype(F32) + qb_in[head:head + 1, :].astype(F32)).astype(BF16)
                q_rows[h, j, rows, :] = block
                q_cols[h, j, :, rows] = block.T
                block = g_in[:, cols]
                g_rows[h, j, rows, :] = block
                g_cols[h, j, :, rows] = block.T
    top[...] = jnp.full(top.shape, NEG, F32)
    total[...] = jnp.zeros(total.shape, F32)
    acc[...] = jnp.zeros(acc.shape, F32)
    q_acc[...] = jnp.zeros(q_acc.shape, F32)
    v_sum[...] = jnp.zeros(v_sum.shape, F32)
    share[...] = jnp.zeros(share.shape, F32)

    position = me * BLOCK + lax.broadcasted_iota(jnp.int32, (1, BLOCK), 1)
    begin = jnp.zeros((1, BLOCK), jnp.int32)
    end = jnp.int32(0)
    for d in range(lens.shape[1]):
        end = end + lens[0, d]
        begin = jnp.where(position >= end, end, begin)

    def forward(c, h):
        near = nearest(c)
        far = jnp.where(c == 0, -1, jnp.where(c == 1, 12, jnp.where(c == 2, 2, 14 - c)))
        offset = lax.broadcasted_iota(jnp.int32, (BLOCK, BLOCK), 0)
        bias = []
        for d in (near, far):
            at = (me - d) * BLOCK + offset
            bias.append(jnp.where((at >= begin) & (at <= position), 0.0, NEG).astype(F32))
        bias = jnp.concatenate(bias, axis=0)
        bias = jnp.concatenate([bias, bias], axis=1)
        pair = kv[pl.ds(2 * c, 2), h]
        keys = pair[:, 0].reshape(2 * BLOCK, HEAD_DIM)
        values_t = pair[:, 1].reshape(2 * BLOCK, HEAD_DIM).T
        for j in range(TILES):
            score = jnp.dot(keys, q_cols[h, j], preferred_element_type=F32) * (SCALE * LOG2E) + bias
            scores[c, h, j] = score
            old = top[h, j]
            new = jnp.maximum(old, jnp.max(score, axis=0, keepdims=True))
            fade = jnp.exp2(old - new)
            weights = jnp.exp2(score - new)
            top[h, j] = new
            total[h, j] = total[h, j] * fade + jnp.sum(weights, axis=0, keepdims=True)
            acc[h, j] = acc[h, j] * fade + jnp.dot(values_t, weights.astype(BF16), preferred_element_type=F32)

    def pass_on(d, h):
        @pl.when(held(d))
        def _():
            for n in range(2):
                ag(d, d, h, n).wait_recv()
                if d in NEXT:
                    to = NEXT[d]
                    if to <= 7:
                        @pl.when(me + 1 < RING)
                        def _():
                            ag(d, to, h, n).start()
                    else:
                        ag(d, to, h, n).start()

    arrivals = {
        2: [(d, h) for h in range(KV) for d in (1, 3, 12)],
        4: [(2, 0)],
        5: [(4, 0), (11, 0), (4, 1), (11, 1), (2, 1)],
        8: [(5, 0), (10, 0)],
        9: [(5, 1), (10, 1)],
        10: [(6, 0), (9, 0)],
        11: [(6, 1), (9, 1)],
        12: [(7, 0), (8, 0)],
        13: [(7, 1), (8, 1)],
    }

    def forward_step(u, _):
        for at, blocks in arrivals.items():
            @pl.when(u == at)
            def _(blocks=blocks):
                for d, h in blocks:
                    pass_on(d, h)

        c = u // 2

        @pl.when(me >= nearest(c))
        def _():
            forward(c, u % 2)

        return 0

    lax.fori_loop(0, CHUNKS * KV, forward_step, 0)

    for h in range(KV):
        for j in range(TILES):
            amount = total[h, j]
            out = (acc[h, j] * (1.0 / amount)).astype(BF16)
            delta[h, j] = jnp.sum(out.astype(F32) * g_cols[h, j].astype(F32), axis=0, keepdims=True)
            top[h, j] = top[h, j] + jnp.log2(amount)
            for e in range(2):
                at = (h * GROUP + j * 2 + e) * 128
                attn_out[:, at:at + 128] = out[:, e * 128:(e + 1) * 128].T

    stores[0].start()

    def backward(c, h):
        pair = kv[pl.ds(2 * c, 2), h]
        keys_t = pair[:, 0].reshape(2 * BLOCK, HEAD_DIM).T
        values = pair[:, 1].reshape(2 * BLOCK, HEAD_DIM)
        v_term = jnp.zeros((2 * BLOCK, HEAD_DIM), F32)
        k_term = jnp.zeros((2 * BLOCK, HEAD_DIM), F32)
        for j in range(TILES):
            probs = jnp.exp2(scores[c, h, j] - top[h, j])
            dprob = jnp.dot(values, g_cols[h, j], preferred_element_type=F32)
            dscore = (probs * (dprob - delta[h, j])).astype(BF16)
            v_term += jnp.dot(probs.astype(BF16), g_rows[h, j], preferred_element_type=F32)
            k_term += jnp.dot(dscore, q_rows[h, j], preferred_element_type=F32)
            q_acc[h, j] += jnp.dot(keys_t, dscore, preferred_element_type=F32)
        terms[pl.ds(2 * c, 2), h, 0] = (k_term * SCALE).reshape(2, BLOCK, HEAD_DIM)
        terms[pl.ds(2 * c, 2), h, 1] = v_term.reshape(2, BLOCK, HEAD_DIM)
        v_sum[h] += jnp.sum(v_term, axis=0, keepdims=True)

    def rs(d, h, n):
        to, step = SUMS[d]
        return remote(sum_out.at[d, h, n], sum_in.at[to, h, n], rs_send.at[d, h, n], rs_recv.at[to, h, n], (dp, z_peer(step), tp))

    def arrived(into, h, n):
        at = sum_in.at[into, h, n]
        remote(at, at, rs_send.at[into, h, n], rs_recv.at[into, h, n], (dp, z_peer(1), tp)).wait_recv()

    def send_sum(d, h):
        def send(mine, before):
            for n in range(2):
                amount = None
                if before:
                    arrived(d, h, n)
                    amount = sum_in[d, h, n]
                if mine:
                    term = terms[SLOT[d], h, n]
                    amount = (term if amount is None else term + amount.astype(F32)).astype(BF16)
                sum_out[d, h, n] = amount
                rs(d, h, n).start()

        if d in (7, 2, 8):
            pl.when(held(d))(lambda: send(True, False))
        elif d <= 7:
            pl.when((me >= d) & (me < RING - 1))(lambda: send(True, True))
            pl.when(me == RING - 1)(lambda: send(True, False))
        else:
            pl.when(me >= d)(lambda: send(True, True))
            pl.when(held(d) & (me < d))(lambda: send(False, True))

    leaving = {h: [(7, h), (8, h)] for h in range(KV)}
    for step, pair in enumerate(((6, 9), (5, 10), (4, 11), (3, 12)), 1):
        for h in range(KV):
            leaving[3 * step + h] = [(d, h) for d in pair]
    leaving[10].append((2, 0))
    leaving[11] = [(2, 1)]

    def backward_step(u, _):
        o = u // 2
        c = 6 - o - (o + 3) // 7 + 2 * ((o + 2) // 7) - (o + 1) // 7

        @pl.when(me >= nearest(c))
        def _():
            backward(c, u % 2)

        for at, sums in leaving.items():
            @pl.when(u == at)
            def _(sums=sums):
                for d, h in sums:
                    send_sum(d, h)

        return 0

    lax.fori_loop(0, CHUNKS * KV, backward_step, 0)

    for h in range(KV):
        for j in range(TILES):
            for e in range(2):
                head = h * GROUP + j * 2 + e
                grad = q_acc[h, j, :, e * 128:(e + 1) * 128].T * SCALE
                share[head:head + 1, :] = jnp.sum(grad, axis=0, keepdims=True)
                qg_out[:, head * 128:(head + 1) * 128] = grad.astype(BF16)
        share[KV * GROUP + h:KV * GROUP + h + 1, :] = v_sum[h]

    stores[1].start()

    def ar_d(o):
        return remote(share, share_d.at[o], ar_send.at[0, o], ar_recv.at[0, o], (d_peer(o), me, tp))

    def ar_z(o):
        return remote(part, share_z.at[o], ar_send.at[1, o], ar_recv.at[1, o], (dp, z_peer(o), tp))

    def each(last, act):
        def body(o, _):
            act(o)
            return 0

        lax.fori_loop(1, last, body, 0)

    def farthest_first(act):
        def body(i, _):
            act(RING // 2 + ((i + 1) // 2) * (1 - 2 * ((i + 1) % 2)))
            return 0

        lax.fori_loop(0, RING - 1, body, 0)

    each(dps, lambda o: ar_d(o).start())
    for h in range(KV):
        send_sum(1, h)
    each(dps, lambda o: ar_d(o).wait_recv())
    share_d[0] = share[...]
    part[...] = jnp.sum(share_d[...], axis=0)
    farthest_first(lambda o: ar_z(o).start())

    for h in range(KV):
        for d, into in ((1, 0), (3, 2), (12, 7)):
            @pl.when(me <= 7 if d == 12 else me + d < RING)
            def _(into=into, h=h):
                for n in range(2):
                    arrived(into, h, n)
                    terms[0, h, n] = terms[0, h, n] + sum_in[into, h, n].astype(F32)
        kg_ref[:, h * 128:(h + 1) * 128] = terms[0, h, 0].astype(BF16)
        vg_ref[:, h * 128:(h + 1) * 128] = terms[0, h, 1].astype(BF16)

    stores[2].start()
    stores[3].start()

    for to in FIRST:
        @pl.when(me <= 7 if to == 12 else me + to < RING)
        def _(to=to):
            for h in range(KV):
                for n in range(2):
                    ag(0, to, h, n).wait_send()
    for d, to in NEXT.items():
        @pl.when(sends(d, to))
        def _(d=d, to=to):
            for h in range(KV):
                for n in range(2):
                    ag(d, to, h, n).wait_send()
    for d in SUMS:
        @pl.when(held(d))
        def _(d=d):
            for h in range(KV):
                for n in range(2):
                    rs(d, h, n).wait_send()
    each(dps, lambda o: ar_d(o).wait_send())

    each(RING, lambda o: ar_z(o).wait_recv())
    share_z[0] = part[...]
    sums = jnp.sum(share_z[...], axis=0) * (1.0 / dps)
    qbg_ref[...] = sums[:KV * GROUP]
    vbg_ref[...] = sums[KV * GROUP:KV * GROUP + KV]
    stores[4].start()
    stores[5].start()
    each(RING, lambda o: ar_z(o).wait_send())
    for copy in stores:
        copy.wait()


def write_out(*refs):
    count = len(refs) // 2
    sem = refs[-1]
    copies = [pltpu.make_async_copy(refs[i], refs[count + i], sem.at[i]) for i in range(count)]
    for copy in copies:
        copy.start()
    for copy in copies:
        copy.wait()


def shards(q_proj, q_bias, k_proj, v_proj, v_bias, dout, lengths):
    width, kv_width = q_proj.shape[2], k_proj.shape[2]
    dps = lax.axis_size("dp")
    hbm = pl.BlockSpec(memory_space=pltpu.HBM)
    block = (KV, 2, BLOCK, HEAD_DIM)
    results = (
        jax.ShapeDtypeStruct((BLOCK, width), BF16),
        jax.ShapeDtypeStruct((BLOCK, width), BF16),
        jax.ShapeDtypeStruct((BLOCK, kv_width), BF16),
        jax.ShapeDtypeStruct((BLOCK, kv_width), BF16),
        jax.ShapeDtypeStruct((KV * GROUP, HEAD_DIM), F32),
        jax.ShapeDtypeStruct((KV, HEAD_DIM), F32),
    )
    held = pl.pallas_call(
        kernel,
        out_shape=results,
        in_specs=[hbm] * 7,
        out_specs=(hbm,) * 6,
        scratch_shapes=[
            *(pltpu.VMEM(result.shape, result.dtype) for result in results),
            pltpu.VMEM((BLOCK, width), BF16),
            pltpu.VMEM((KV * GROUP, HEAD_DIM), BF16),
            pltpu.VMEM((BLOCK, kv_width), BF16),
            pltpu.VMEM((BLOCK, kv_width), BF16),
            pltpu.VMEM((KV, HEAD_DIM), BF16),
            pltpu.VMEM((BLOCK, width), BF16),
            pltpu.SMEM(lengths.shape, jnp.int32),
            pltpu.VMEM((KV, TILES, 2 * BLOCK, HEAD_DIM), BF16),
            pltpu.VMEM((KV, TILES, 2 * BLOCK, HEAD_DIM), BF16),
            pltpu.VMEM((KV, TILES, HEAD_DIM, 2 * BLOCK), BF16),
            pltpu.VMEM((KV, TILES, HEAD_DIM, 2 * BLOCK), BF16),
            pltpu.VMEM((2 * CHUNKS,) + block, BF16),
            pltpu.VMEM((CHUNKS, KV, TILES, 2 * BLOCK, 2 * BLOCK), F32),
            pltpu.VMEM((KV, TILES, 1, 2 * BLOCK), F32),
            pltpu.VMEM((KV, TILES, 1, 2 * BLOCK), F32),
            pltpu.VMEM((KV, TILES, 1, 2 * BLOCK), F32),
            pltpu.VMEM((KV, TILES, HEAD_DIM, 2 * BLOCK), F32),
            pltpu.VMEM((KV, TILES, HEAD_DIM, 2 * BLOCK), F32),
            pltpu.VMEM((2 * CHUNKS,) + block, F32),
            pltpu.VMEM((KV, 1, HEAD_DIM), F32),
            pltpu.VMEM((13,) + block, BF16),
            pltpu.VMEM((13,) + block, BF16),
            pltpu.VMEM((ROWS, HEAD_DIM), F32),
            pltpu.VMEM((dps, ROWS, HEAD_DIM), F32),
            pltpu.VMEM((ROWS, HEAD_DIM), F32),
            pltpu.VMEM((RING, ROWS, HEAD_DIM), F32),
            pltpu.SemaphoreType.DMA((7,)),
            pltpu.SemaphoreType.DMA((6,)),
            pltpu.SemaphoreType.DMA((13, KV, 2)),
            pltpu.SemaphoreType.DMA((13, KV, 2)),
            pltpu.SemaphoreType.DMA((13, KV, 2)),
            pltpu.SemaphoreType.DMA((13, KV, 2)),
            pltpu.SemaphoreType.DMA((2, RING)),
            pltpu.SemaphoreType.DMA((2, RING)),
        ],
        compiler_params=pltpu.CompilerParams(
            collective_id=0, has_side_effects=True, vmem_limit_bytes=60 * 2**20
        ),
        cost_estimate=pl.CostEstimate(flops=6 * 10**9, bytes_accessed=3 * 10**6, transcendentals=7 * 10**6),
        name="attention",
    )(
        q_proj[0],
        q_bias.reshape(-1, HEAD_DIM),
        k_proj[0],
        v_proj[0],
        v_bias.reshape(-1, HEAD_DIM),
        dout[0],
        lengths,
    )
    attn, q_grad, k_grad, v_grad, q_sums, v_sums = pl.pallas_call(
        write_out,
        out_shape=results,
        in_specs=[hbm] * 6,
        out_specs=(hbm,) * 6,
        scratch_shapes=[pltpu.SemaphoreType.DMA((6,))],
        compiler_params=pltpu.CompilerParams(vmem_limit_bytes=60 * 2**20),
        name="write_out",
    )(*held)
    return attn[None], q_grad[None], k_grad[None], v_grad[None], q_sums.reshape(-1), v_sums.reshape(-1)


def solution(mesh):
    placed = (
        P("dp", "ctx", "tp"),
        P("tp"),
        P("dp", "ctx", "tp"),
        P("dp", "ctx", "tp"),
        P("tp"),
        P("dp", "ctx", "tp"),
        P("dp", None),
    )
    return jax.shard_map(
        shards,
        mesh=mesh,
        in_specs=placed,
        out_specs=(
            P("dp", "ctx", "tp"),
            P("dp", "ctx", "tp"),
            P("dp", "ctx", "tp"),
            P("dp", "ctx", "tp"),
            P("tp"),
            P("tp"),
        ),
        check_vma=False,
    )
```

```python
import math

import jax
import jax.numpy as jnp
from jax import lax
from jax.experimental import pallas as pl
from jax.experimental.pallas import tpu as pltpu
from jax.sharding import PartitionSpec as P

HEAD_DIM = 128
SCALE = HEAD_DIM ** -0.5
LOG2E = math.log2(math.e)
NEG = -1e30
BLOCK = 128
KV = 2
GROUP = 8
TILES = 4
RING = 16
CHUNKS = 7
F32 = jnp.float32
BF16 = jnp.bfloat16

PAIRS = ((0, None), (3, 12), (1, 2), (4, 11), (5, 10), (6, 9), (7, 8))
SLOT = {d: 2 * c + n for c, pair in enumerate(PAIRS) for n, d in enumerate(pair) if d is not None}
NEXT = {1: 2, 3: 4, 4: 5, 5: 6, 6: 7, 12: 11, 11: 10, 10: 9, 9: 8}
FIRST = (12, 3, 1)
SUMS = {7: (6, -1), 6: (5, -1), 5: (4, -1), 4: (3, -1), 3: (2, -3), 2: (1, -1), 1: (0, -1),
        8: (9, 1), 9: (10, 1), 10: (11, 1), 11: (12, 1), 12: (7, 4)}
STEPS = (1, -1, 3, -3, 4, -4)
ROWS = 24


def nearest(c):
    return 3 * ((c + 6) // 7) - 2 * ((c + 5) // 7) + c * ((c + 4) // 7)


def kernel(
    q_hbm, qb_hbm, k_hbm, v_hbm, vb_hbm, g_hbm, len_hbm,
    attn_hbm, qg_hbm, kg_hbm, vg_hbm, qbg_hbm, vbg_hbm,
    attn_out, qg_out, kg_ref, vg_ref, qbg_ref, vbg_ref, q_in, qb_in, k_in, v_in, vb_in, g_in, lens, q_rows, g_rows, q_cols, g_cols, kv, scores, top, total, delta, acc, q_acc, terms, attn_t, probs_b, dscores,
    v_sum, sum_in, sum_out, share, share_d, part, share_z,
    load_sem, store_sem, ag_send, ag_recv, rs_send, rs_recv, ar_send, ar_recv,
):
    dp, me, tp = lax.axis_index("dp"), lax.axis_index("ctx"), lax.axis_index("tp")
    dps = lax.axis_size("dp")

    def z_peer(o):
        return lax.rem(me + RING + o, RING)

    def d_peer(o):
        return lax.rem(dp + o, dps)

    loads = [
        pltpu.make_async_copy(src, dst, load_sem.at[i])
        for i, (src, dst) in enumerate((
            (k_hbm, k_in), (v_hbm, v_in), (vb_hbm, vb_in), (q_hbm, q_in), (g_hbm, g_in), (qb_hbm, qb_in), (len_hbm, lens)))
    ]
    for copy in loads:
        copy.start()

    stores = [
        pltpu.make_async_copy(src, dst, store_sem.at[i])
        for i, (src, dst) in enumerate((
            (attn_out, attn_hbm), (qg_out, qg_hbm), (kg_ref, kg_hbm), (vg_ref, vg_hbm), (qbg_ref, qbg_hbm), (vbg_ref, vbg_hbm)))
    ]
    barrier = pltpu.get_barrier_semaphore()

    for step in STEPS:
        pl.semaphore_signal(barrier, inc=1, device_id=(dp, z_peer(step), tp), device_id_type=pl.DeviceIdType.MESH)

    def greet_d(o, _):
        pl.semaphore_signal(barrier, inc=1, device_id=(d_peer(o), me, tp), device_id_type=pl.DeviceIdType.MESH)
        return 0

    lax.fori_loop(1, dps, greet_d, 0)

    def remote(src, dst, send, recv, device):
        return pltpu.make_async_remote_copy(
            src_ref=src, dst_ref=dst, send_sem=send, recv_sem=recv, device_id=device, device_id_type=pl.DeviceIdType.MESH
        )

    def held(d):
        return me >= d if d <= 7 else lax.rem(me + RING - d, RING) <= 7

    def ag(d, to, h, n):
        step = to - d if to <= 7 else (-4 if d == 0 else -1)
        return remote(kv.at[SLOT[d], h, n], kv.at[SLOT[to], h, n], ag_send.at[to, h, n], ag_recv.at[to, h, n], (dp, z_peer(step), tp))

    def sends(d, to):
        return (held(d) & (me + to - d < RING)) if to <= 7 else held(d)

    for copy in loads[:3]:
        copy.wait()
    for h in range(KV):
        cols = slice(h * 128, (h + 1) * 128)
        kv[0, h, 0] = k_in[:, cols]
        kv[0, h, 1] = (v_in[:, cols].astype(F32) + vb_in[h:h + 1, :].astype(F32)).astype(BF16)
    nothing = jnp.zeros((KV, 2, BLOCK, HEAD_DIM), BF16)
    kv[1] = nothing
    pl.semaphore_wait(barrier, len(STEPS) + dps - 1)
    for to in FIRST:
        @pl.when(me <= 7 if to == 12 else me + to < RING)
        def _(to=to):
            for h in range(KV):
                for n in range(2):
                    ag(0, to, h, n).start()

    for d in (2, 8, 9, 10, 11, 12):
        @pl.when(jnp.logical_not(held(d)))
        def _(d=d):
            kv[SLOT[d]] = nothing

    for copy in loads[3:]:
        copy.wait()
    for h in range(KV):
        for j in range(TILES):
            for e in range(2):
                head = h * GROUP + j * 2 + e
                cols = slice(head * 128, (head + 1) * 128)
                rows = slice(e * 128, (e + 1) * 128)
                block = (q_in[:, cols].astype(F32) + qb_in[head:head + 1, :].astype(F32)).astype(BF16)
                q_rows[h, j, rows, :] = block
                q_cols[h, j, :, rows] = block.T
                block = g_in[:, cols]
                g_rows[h, j, rows, :] = block
                g_cols[h, j, :, rows] = block.T
    top[...] = jnp.full(top.shape, NEG, F32)
    total[...] = jnp.zeros(total.shape, F32)
    acc[...] = jnp.zeros(acc.shape, F32)
    q_acc[...] = jnp.zeros(q_acc.shape, F32)
    v_sum[...] = jnp.zeros(v_sum.shape, F32)
    share[...] = jnp.zeros(share.shape, F32)

    position = me * BLOCK + lax.broadcasted_iota(jnp.int32, (1, BLOCK), 1)
    begin = jnp.zeros((1, BLOCK), jnp.int32)
    end = jnp.int32(0)
    for d in range(lens.shape[1]):
        end = end + lens[0, d]
        begin = jnp.where(position >= end, end, begin)

    def forward(c, h):
        near = nearest(c)
        far = jnp.where(c == 0, -1, jnp.where(c == 1, 12, jnp.where(c == 2, 2, 14 - c)))
        offset = lax.broadcasted_iota(jnp.int32, (BLOCK, BLOCK), 0)
        bias = []
        for d in (near, far):
            at = (me - d) * BLOCK + offset
            bias.append(jnp.where((at >= begin) & (at <= position), 0.0, NEG).astype(F32))
        bias = jnp.concatenate(bias, axis=0)
        pair = kv[pl.ds(2 * c, 2), h]
        keys = pair[:, 0].reshape(2 * BLOCK, HEAD_DIM)
        values_t = pair[:, 1].reshape(2 * BLOCK, HEAD_DIM).T
        for j in range(TILES):
            for e in range(2):
                at = slice(e * 128, (e + 1) * 128)
                score = jnp.dot(keys, q_cols[h, j, :, at], preferred_element_type=F32) * (SCALE * LOG2E) + bias
                scores[c, h, j, :, at] = score
                old = top[h, j, :, at]
                new = jnp.maximum(old, jnp.max(score, axis=0, keepdims=True))
                fade = jnp.exp2(old - new)
                weights = jnp.exp2(score - new)
                top[h, j, :, at] = new
                total[h, j, :, at] = total[h, j, :, at] * fade + jnp.sum(weights, axis=0, keepdims=True)
                acc[h, j, :, at] = acc[h, j, :, at] * fade + jnp.dot(
                    values_t, weights.astype(BF16), preferred_element_type=F32)

    def pass_on(d, h):
        @pl.when(held(d))
        def _():
            for n in range(2):
                ag(d, d, h, n).wait_recv()
                if d in NEXT:
                    to = NEXT[d]
                    if to <= 7:
                        @pl.when(me + 1 < RING)
                        def _():
                            ag(d, to, h, n).start()
                    else:
                        ag(d, to, h, n).start()

    arrivals = {
        2: [(d, h) for h in range(KV) for d in (1, 3, 12)],
        4: [(2, 0)],
        5: [(4, 0), (11, 0), (4, 1), (11, 1), (2, 1)],
        8: [(5, 0), (10, 0), (5, 1), (10, 1)],
        10: [(6, 0), (9, 0), (6, 1), (9, 1)],
        12: [(7, 0), (8, 0)],
        13: [(7, 1), (8, 1)],
    }

    def forward_step(u, _):
        for at, blocks in arrivals.items():
            @pl.when(u == at)
            def _(blocks=blocks):
                for d, h in blocks:
                    pass_on(d, h)

        c = u // 2

        @pl.when(me >= nearest(c))
        def _():
            forward(c, u % 2)

        return 0

    lax.fori_loop(0, CHUNKS * KV, forward_step, 0)

    for h in range(KV):
        for j in range(TILES):
            amount = total[h, j]
            out = (acc[h, j] * (1.0 / amount)).astype(BF16)
            delta[h, j] = jnp.sum(out.astype(F32) * g_cols[h, j].astype(F32), axis=0, keepdims=True)
            top[h, j] = top[h, j] + jnp.log2(amount)
            attn_t[h, j] = out

    def write_attention():
        for h in range(KV):
            for j in range(TILES):
                for e in range(2):
                    at = (h * GROUP + j * 2 + e) * 128
                    attn_out[:, at:at + 128] = attn_t[h, j, :, e * 128:(e + 1) * 128].T
        stores[0].start()

    def backward(c, h):
        pair = kv[pl.ds(2 * c, 2), h]
        keys_t = pair[:, 0].reshape(2 * BLOCK, HEAD_DIM).T
        values = pair[:, 1].reshape(2 * BLOCK, HEAD_DIM)
        for j in range(TILES):
            at = slice(j * 256, (j + 1) * 256)
            probs = jnp.exp2(scores[c, h, j] - top[h, j])
            dprob = jnp.dot(values, g_cols[h, j], preferred_element_type=F32)
            dscores[:, at] = (probs * (dprob - delta[h, j])).astype(BF16)
            probs_b[:, at] = probs.astype(BF16)
        v_term = jnp.dot(probs_b[...], g_rows[h].reshape(GROUP * BLOCK, HEAD_DIM), preferred_element_type=F32)
        k_term = jnp.dot(dscores[...], q_rows[h].reshape(GROUP * BLOCK, HEAD_DIM), preferred_element_type=F32)
        q_term = jnp.dot(keys_t, dscores[...], preferred_element_type=F32)
        for j in range(TILES):
            q_acc[h, j] += q_term[:, j * 256:(j + 1) * 256]
        terms[pl.ds(2 * c, 2), h, 0] = (k_term * SCALE).reshape(2, BLOCK, HEAD_DIM)
        terms[pl.ds(2 * c, 2), h, 1] = v_term.reshape(2, BLOCK, HEAD_DIM)
        v_sum[h] += jnp.sum(v_term, axis=0, keepdims=True)

    def rs(d, h, n):
        to, step = SUMS[d]
        return remote(sum_out.at[d, h, n], sum_in.at[to, h, n], rs_send.at[d, h, n], rs_recv.at[to, h, n], (dp, z_peer(step), tp))

    def arrived(into, h, n):
        at = sum_in.at[into, h, n]
        remote(at, at, rs_send.at[into, h, n], rs_recv.at[into, h, n], (dp, z_peer(1), tp)).wait_recv()

    def send_sum(d, h):
        def send(mine, before):
            for n in range(2):
                amount = None
                if before:
                    arrived(d, h, n)
                    amount = sum_in[d, h, n]
                if mine:
                    term = terms[SLOT[d], h, n]
                    amount = (term if amount is None else term + amount.astype(F32)).astype(BF16)
                sum_out[d, h, n] = amount
                rs(d, h, n).start()

        if d in (7, 2, 8):
            pl.when(held(d))(lambda: send(True, False))
        elif d <= 7:
            pl.when((me >= d) & (me < RING - 1))(lambda: send(True, True))
            pl.when(me == RING - 1)(lambda: send(True, False))
        else:
            pl.when(me >= d)(lambda: send(True, True))
            pl.when(held(d) & (me < d))(lambda: send(False, True))

    leaving = {
        0: [(7, 0), (8, 0)],
        1: [(7, 1), (8, 1)],
        6: [(6, 0), (9, 0)],
        7: [(6, 1), (9, 1)],
        11: [(2, 0), (2, 1)],
        12: [(5, 0), (10, 0)],
        13: [(5, 1), (10, 1)],
    }

    def backward_step(u, _):
        o = u // 2
        c = 6 - o - (o + 3) // 7 + 2 * ((o + 2) // 7) - (o + 1) // 7

        @pl.when(me >= nearest(c))
        def _():
            backward(c, u % 2)

        pl.when(u == 2)(write_attention)

        for at, sums in leaving.items():
            @pl.when(u == at)
            def _(sums=sums):
                for d, h in sums:
                    send_sum(d, h)

        return 0

    lax.fori_loop(0, CHUNKS * KV, backward_step, 0)

    for h in range(KV):
        for j in range(TILES):
            for e in range(2):
                head = h * GROUP + j * 2 + e
                grad = q_acc[h, j, :, e * 128:(e + 1) * 128].T * SCALE
                share[head:head + 1, :] = jnp.sum(grad, axis=0, keepdims=True)
                qg_out[:, head * 128:(head + 1) * 128] = grad.astype(BF16)
        share[KV * GROUP + h:KV * GROUP + h + 1, :] = v_sum[h]

    stores[1].start()

    def ar_d(o):
        return remote(share, share_d.at[o], ar_send.at[0, o], ar_recv.at[0, o], (d_peer(o), me, tp))

    def ar_z(o):
        return remote(part, share_z.at[o], ar_send.at[1, o], ar_recv.at[1, o], (dp, z_peer(o), tp))

    def each(last, act):
        def body(o, _):
            act(o)
            return 0

        lax.fori_loop(1, last, body, 0)

    def farthest_first(act):
        def body(i, _):
            act(RING // 2 + ((i + 1) // 2) * (1 - 2 * ((i + 1) % 2)))
            return 0

        lax.fori_loop(0, RING - 1, body, 0)

    each(dps, lambda o: ar_d(o).start())
    for h in range(KV):
        send_sum(4, h)
        send_sum(11, h)
    each(dps, lambda o: ar_d(o).wait_recv())
    share_d[0] = share[...]
    part[...] = jnp.sum(share_d[...], axis=0)
    farthest_first(lambda o: ar_z(o).start())
    for h in range(KV):
        send_sum(3, h)
        send_sum(12, h)
    for h in range(KV):
        send_sum(1, h)

    for h in range(KV):
        for d, into in ((1, 0), (3, 2), (12, 7)):
            @pl.when(me <= 7 if d == 12 else me + d < RING)
            def _(into=into, h=h):
                for n in range(2):
                    arrived(into, h, n)
                    terms[0, h, n] = terms[0, h, n] + sum_in[into, h, n].astype(F32)
        kg_ref[:, h * 128:(h + 1) * 128] = terms[0, h, 0].astype(BF16)
        vg_ref[:, h * 128:(h + 1) * 128] = terms[0, h, 1].astype(BF16)

    stores[2].start()
    stores[3].start()

    for to in FIRST:
        @pl.when(me <= 7 if to == 12 else me + to < RING)
        def _(to=to):
            for h in range(KV):
                for n in range(2):
                    ag(0, to, h, n).wait_send()
    for d, to in NEXT.items():
        @pl.when(sends(d, to))
        def _(d=d, to=to):
            for h in range(KV):
                for n in range(2):
                    ag(d, to, h, n).wait_send()
    for d in SUMS:
        @pl.when(held(d))
        def _(d=d):
            for h in range(KV):
                for n in range(2):
                    rs(d, h, n).wait_send()
    each(dps, lambda o: ar_d(o).wait_send())

    each(RING, lambda o: ar_z(o).wait_recv())
    share_z[0] = part[...]
    sums = jnp.sum(share_z[...], axis=0) * (1.0 / dps)
    qbg_ref[...] = sums[:KV * GROUP]
    vbg_ref[...] = sums[KV * GROUP:KV * GROUP + KV]
    stores[4].start()
    stores[5].start()
    each(RING, lambda o: ar_z(o).wait_send())
    for copy in stores:
        copy.wait()


def write_out(*refs):
    count = 6
    sources, results, held = refs[:count], refs[count:2 * count], refs[2 * count:3 * count]
    sem_in, sem_out = refs[3 * count:]
    parts = []
    for i in range(count):
        rows = sources[i].shape[0]
        step = 32 if rows == BLOCK else rows
        parts += [(i, pl.ds(at, step)) for at in range(0, rows, step)]
    ins = [pltpu.make_async_copy(sources[i].at[at], held[i].at[at], sem_in.at[n]) for n, (i, at) in enumerate(parts)]
    outs = [pltpu.make_async_copy(held[i].at[at], results[i].at[at], sem_out.at[n]) for n, (i, at) in enumerate(parts)]
    for copy in ins:
        copy.start()
    for copy, onward in zip(ins, outs):
        copy.wait()
        onward.start()
    for copy in outs:
        copy.wait()


def shards(q_proj, q_bias, k_proj, v_proj, v_bias, dout, lengths):
    width, kv_width = q_proj.shape[2], k_proj.shape[2]
    dps = lax.axis_size("dp")
    hbm = pl.BlockSpec(memory_space=pltpu.HBM)
    block = (KV, 2, BLOCK, HEAD_DIM)
    results = (
        jax.ShapeDtypeStruct((BLOCK, width), BF16),
        jax.ShapeDtypeStruct((BLOCK, width), BF16),
        jax.ShapeDtypeStruct((BLOCK, kv_width), BF16),
        jax.ShapeDtypeStruct((BLOCK, kv_width), BF16),
        jax.ShapeDtypeStruct((KV * GROUP, HEAD_DIM), F32),
        jax.ShapeDtypeStruct((KV, HEAD_DIM), F32),
    )
    held = pl.pallas_call(
        kernel,
        out_shape=results,
        in_specs=[hbm] * 7,
        out_specs=(hbm,) * 6,
        scratch_shapes=[
            *(pltpu.VMEM(result.shape, result.dtype) for result in results),
            pltpu.VMEM((BLOCK, width), BF16),
            pltpu.VMEM((KV * GROUP, HEAD_DIM), BF16),
            pltpu.VMEM((BLOCK, kv_width), BF16),
            pltpu.VMEM((BLOCK, kv_width), BF16),
            pltpu.VMEM((KV, HEAD_DIM), BF16),
            pltpu.VMEM((BLOCK, width), BF16),
            pltpu.SMEM(lengths.shape, jnp.int32),
            pltpu.VMEM((KV, TILES, 2 * BLOCK, HEAD_DIM), BF16),
            pltpu.VMEM((KV, TILES, 2 * BLOCK, HEAD_DIM), BF16),
            pltpu.VMEM((KV, TILES, HEAD_DIM, 2 * BLOCK), BF16),
            pltpu.VMEM((KV, TILES, HEAD_DIM, 2 * BLOCK), BF16),
            pltpu.VMEM((2 * CHUNKS,) + block, BF16),
            pltpu.VMEM((CHUNKS, KV, TILES, 2 * BLOCK, 2 * BLOCK), F32),
            pltpu.VMEM((KV, TILES, 1, 2 * BLOCK), F32),
            pltpu.VMEM((KV, TILES, 1, 2 * BLOCK), F32),
            pltpu.VMEM((KV, TILES, 1, 2 * BLOCK), F32),
            pltpu.VMEM((KV, TILES, HEAD_DIM, 2 * BLOCK), F32),
            pltpu.VMEM((KV, TILES, HEAD_DIM, 2 * BLOCK), F32),
            pltpu.VMEM((2 * CHUNKS,) + block, F32),
            pltpu.VMEM((KV, TILES, HEAD_DIM, 2 * BLOCK), BF16),
            pltpu.VMEM((2 * BLOCK, GROUP * BLOCK), BF16),
            pltpu.VMEM((2 * BLOCK, GROUP * BLOCK), BF16),
            pltpu.VMEM((KV, 1, HEAD_DIM), F32),
            pltpu.VMEM((13,) + block, BF16),
            pltpu.VMEM((13,) + block, BF16),
            pltpu.VMEM((ROWS, HEAD_DIM), F32),
            pltpu.VMEM((dps, ROWS, HEAD_DIM), F32),
            pltpu.VMEM((ROWS, HEAD_DIM), F32),
            pltpu.VMEM((RING, ROWS, HEAD_DIM), F32),
            pltpu.SemaphoreType.DMA((7,)),
            pltpu.SemaphoreType.DMA((6,)),
            pltpu.SemaphoreType.DMA((13, KV, 2)),
            pltpu.SemaphoreType.DMA((13, KV, 2)),
            pltpu.SemaphoreType.DMA((13, KV, 2)),
            pltpu.SemaphoreType.DMA((13, KV, 2)),
            pltpu.SemaphoreType.DMA((2, RING)),
            pltpu.SemaphoreType.DMA((2, RING)),
        ],
        compiler_params=pltpu.CompilerParams(
            collective_id=0, has_side_effects=True, vmem_limit_bytes=60 * 2**20
        ),
        cost_estimate=pl.CostEstimate(flops=6 * 10**9, bytes_accessed=3 * 10**6, transcendentals=7 * 10**6),
        name="attention",
    )(
        q_proj[0],
        q_bias.reshape(-1, HEAD_DIM),
        k_proj[0],
        v_proj[0],
        v_bias.reshape(-1, HEAD_DIM),
        dout[0],
        lengths,
    )
    attn, q_grad, k_grad, v_grad, q_sums, v_sums = pl.pallas_call(
        write_out,
        out_shape=results,
        in_specs=[hbm] * 6,
        out_specs=(hbm,) * 6,
        scratch_shapes=[
            *(pltpu.VMEM(result.shape, result.dtype) for result in results),
            pltpu.SemaphoreType.DMA((18,)),
            pltpu.SemaphoreType.DMA((18,)),
        ],
        compiler_params=pltpu.CompilerParams(vmem_limit_bytes=60 * 2**20),
        name="write_out",
    )(*held)
    return attn[None], q_grad[None], k_grad[None], v_grad[None], q_sums.reshape(-1), v_sums.reshape(-1)


def solution(mesh):
    placed = (
        P("dp", "ctx", "tp"),
        P("tp"),
        P("dp", "ctx", "tp"),
        P("dp", "ctx", "tp"),
        P("tp"),
        P("dp", "ctx", "tp"),
        P("dp", None),
    )
    return jax.shard_map(
        shards,
        mesh=mesh,
        in_specs=placed,
        out_specs=(
            P("dp", "ctx", "tp"),
            P("dp", "ctx", "tp"),
            P("dp", "ctx", "tp"),
            P("dp", "ctx", "tp"),
            P("tp"),
            P("tp"),
        ),
        check_vma=False,
    )
```

```python
import math

import jax
import jax.numpy as jnp
from jax import lax
from jax.experimental import pallas as pl
from jax.experimental.pallas import tpu as pltpu
from jax.sharding import PartitionSpec as P

HEAD_DIM = 128
SCALE = HEAD_DIM ** -0.5
LOG2E = math.log2(math.e)
NEG = -1e30
BLOCK = 128
KV = 2
GROUP = 8
TILES = 4
RING = 16
CHUNKS = 7
F32 = jnp.float32
BF16 = jnp.bfloat16

PAIRS = ((0, None), (3, 12), (4, 11), (1, 2), (5, 10), (6, 9), (7, 8))
SLOT = {d: 2 * c + n for c, pair in enumerate(PAIRS) for n, d in enumerate(pair) if d is not None}
NEXT = {1: 2, 3: 4, 4: 5, 5: 6, 6: 7, 12: 11, 11: 10, 10: 9, 9: 8}
FIRST = (12, 3, 1)
UNITS = 2 * CHUNKS * KV
SUMS = {7: (6, -1), 6: (5, -1), 5: (4, -1), 4: (3, -1), 3: (2, -3), 2: (1, -1), 1: (0, -1),
        8: (9, 1), 9: (10, 1), 10: (11, 1), 11: (12, 1), 12: (7, 4)}
STEPS = (1, -1, 3, -3, 4, -4)
ROWS = 2 * KV * GROUP


def nearest(c):
    return (c + 2) * ((c + 6) // 7) - 4 * ((c + 4) // 7) + 3 * ((c + 3) // 7)


def kernel(
    q_hbm, qb_hbm, k_hbm, v_hbm, vb_hbm, g_hbm, len_hbm,
    attn_hbm, qg_hbm, kg_hbm, vg_hbm, qbg_hbm, vbg_hbm,
    attn_out, qg_out, kg_ref, vg_ref, qbg_ref, vbg_ref, q_in, qb_in, k_in, v_in, vb_in, g_in, lens, q_rows, g_rows, q_cols, g_cols, kv, scores, top, total, delta, acc, q_acc, terms, attn_t, probs_b, dscores,
    v_sum, sum_in, sum_out, share, share_d, part, share_z, sums,
    load_sem, store_sem, ag_send, ag_recv, rs_send, rs_recv, ar_send, ar_recv,
):
    dp, me, tp = lax.axis_index("dp"), lax.axis_index("ctx"), lax.axis_index("tp")
    dps = lax.axis_size("dp")

    def z_peer(o):
        return lax.rem(me + RING + o, RING)

    def d_peer(o):
        return lax.rem(dp + o, dps)

    loads = [
        pltpu.make_async_copy(src, dst, load_sem.at[i])
        for i, (src, dst) in enumerate((
            (k_hbm, k_in), (v_hbm, v_in), (vb_hbm, vb_in), (q_hbm, q_in), (g_hbm, g_in), (qb_hbm, qb_in), (len_hbm, lens)))
    ]
    for copy in loads:
        copy.start()

    stores = [
        pltpu.make_async_copy(src, dst, store_sem.at[i])
        for i, (src, dst) in enumerate((
            (attn_out, attn_hbm), (qg_out, qg_hbm), (kg_ref, kg_hbm), (vg_ref, vg_hbm), (qbg_ref, qbg_hbm), (vbg_ref, vbg_hbm)))
    ]
    barrier = pltpu.get_barrier_semaphore()

    for step in STEPS:
        pl.semaphore_signal(barrier, inc=1, device_id=(dp, z_peer(step), tp), device_id_type=pl.DeviceIdType.MESH)

    def greet_d(o, _):
        pl.semaphore_signal(barrier, inc=1, device_id=(d_peer(o), me, tp), device_id_type=pl.DeviceIdType.MESH)
        return 0

    lax.fori_loop(1, dps, greet_d, 0)

    def remote(src, dst, send, recv, device):
        return pltpu.make_async_remote_copy(
            src_ref=src, dst_ref=dst, send_sem=send, recv_sem=recv, device_id=device, device_id_type=pl.DeviceIdType.MESH
        )

    def held(d):
        return me >= d if d <= 7 else lax.rem(me + RING - d, RING) <= 7

    def ag(d, to, h, n):
        step = to - d if to <= 7 else (-4 if d == 0 else -1)
        return remote(kv.at[SLOT[d], h, n], kv.at[SLOT[to], h, n], ag_send.at[to, h, n], ag_recv.at[to, h, n], (dp, z_peer(step), tp))

    def sends(d, to):
        return (held(d) & (me + to - d < RING)) if to <= 7 else held(d)

    for copy in loads[:3]:
        copy.wait()
    for h in range(KV):
        cols = slice(h * 128, (h + 1) * 128)
        kv[0, h, 0] = k_in[:, cols]
        kv[0, h, 1] = (v_in[:, cols].astype(F32) + vb_in[h:h + 1, :].astype(F32)).astype(BF16)
    nothing = jnp.zeros((KV, 2, BLOCK, HEAD_DIM), BF16)
    kv[1] = nothing
    pl.semaphore_wait(barrier, len(STEPS) + dps - 1)

    def send_own(to, h):
        @pl.when(me <= 7 if to == 12 else me + to < RING)
        def _():
            for n in range(2):
                ag(0, to, h, n).start()

    for h in range(KV):
        send_own(12, h)
        send_own(3, h)

    for d in (2, 8, 9, 10, 11, 12):
        @pl.when(jnp.logical_not(held(d)))
        def _(d=d):
            kv[SLOT[d]] = nothing

    for copy in loads[3:]:
        copy.wait()
    for h in range(KV):
        for j in range(TILES):
            for e in range(2):
                head = h * GROUP + j * 2 + e
                cols = slice(head * 128, (head + 1) * 128)
                rows = slice(e * 128, (e + 1) * 128)
                block = (q_in[:, cols].astype(F32) + qb_in[head:head + 1, :].astype(F32)).astype(BF16)
                q_rows[h, j, rows, :] = block
                q_cols[h, j, :, rows] = block.T
                block = g_in[:, cols]
                g_rows[h, j, rows, :] = block
                g_cols[h, j, :, rows] = block.T
    top[...] = jnp.full(top.shape, NEG, F32)
    total[...] = jnp.zeros(total.shape, F32)
    acc[...] = jnp.zeros(acc.shape, F32)
    q_acc[...] = jnp.zeros(q_acc.shape, F32)
    v_sum[...] = jnp.zeros(v_sum.shape, F32)
    share[...] = jnp.zeros(share.shape, F32)

    position = me * BLOCK + lax.broadcasted_iota(jnp.int32, (1, BLOCK), 1)
    begin = jnp.zeros((1, BLOCK), jnp.int32)
    end = jnp.int32(0)
    for d in range(lens.shape[1]):
        end = end + lens[0, d]
        begin = jnp.where(position >= end, end, begin)

    def forward(c, h):
        near = nearest(c)
        far = jnp.where(c == 0, -1, jnp.where(c == 3, 2, jnp.where(c <= 2, 13 - c, 14 - c)))
        offset = lax.broadcasted_iota(jnp.int32, (BLOCK, BLOCK), 0)
        bias = []
        for d in (near, far):
            at = (me - d) * BLOCK + offset
            bias.append(jnp.where((at >= begin) & (at <= position), 0.0, NEG).astype(F32))
        bias = jnp.concatenate(bias, axis=0)
        pair = kv[pl.ds(2 * c, 2), h]
        keys = pair[:, 0].reshape(2 * BLOCK, HEAD_DIM)
        values_t = pair[:, 1].reshape(2 * BLOCK, HEAD_DIM).T
        for j in range(TILES):
            for e in range(2):
                at = slice(e * 128, (e + 1) * 128)
                score = jnp.dot(keys, q_cols[h, j, :, at], preferred_element_type=F32) * (SCALE * LOG2E) + bias
                scores[c, h, j, :, at] = score
                old = top[h, j, :, at]
                new = jnp.maximum(old, jnp.max(score, axis=0, keepdims=True))
                fade = jnp.exp2(old - new)
                weights = jnp.exp2(score - new)
                top[h, j, :, at] = new
                total[h, j, :, at] = total[h, j, :, at] * fade + jnp.sum(weights, axis=0, keepdims=True)
                acc[h, j, :, at] = acc[h, j, :, at] * fade + jnp.dot(
                    values_t, weights.astype(BF16), preferred_element_type=F32)

    def pass_on(d, h):
        @pl.when(held(d))
        def _():
            for n in range(2):
                ag(d, d, h, n).wait_recv()
                if d in NEXT:
                    to = NEXT[d]
                    if to <= 7:
                        @pl.when(me + 1 < RING)
                        def _():
                            ag(d, to, h, n).start()
                    else:
                        ag(d, to, h, n).start()

    def finish(h):
        for j in range(TILES):
            amount = total[h, j]
            out = (acc[h, j] * (1.0 / amount)).astype(BF16)
            delta[h, j] = jnp.sum(out.astype(F32) * g_cols[h, j].astype(F32), axis=0, keepdims=True)
            top[h, j] = top[h, j] + jnp.log2(amount)
            attn_t[h, j] = out

    def write_attention():
        for h in range(KV):
            for j in range(TILES):
                for e in range(2):
                    at = (h * GROUP + j * 2 + e) * 128
                    attn_out[:, at:at + 128] = attn_t[h, j, :, e * 128:(e + 1) * 128].T
        stores[0].start()

    def backward(c, h):
        pair = kv[pl.ds(2 * c, 2), h]
        keys_t = pair[:, 0].reshape(2 * BLOCK, HEAD_DIM).T
        values = pair[:, 1].reshape(2 * BLOCK, HEAD_DIM)
        for j in range(TILES):
            at = slice(j * 256, (j + 1) * 256)
            probs = jnp.exp2(scores[c, h, j] - top[h, j])
            dprob = jnp.dot(values, g_cols[h, j], preferred_element_type=F32)
            dscores[:, at] = (probs * (dprob - delta[h, j])).astype(BF16)
            probs_b[:, at] = probs.astype(BF16)
        v_term = jnp.dot(probs_b[...], g_rows[h].reshape(GROUP * BLOCK, HEAD_DIM), preferred_element_type=F32)
        k_term = jnp.dot(dscores[...], q_rows[h].reshape(GROUP * BLOCK, HEAD_DIM), preferred_element_type=F32)
        q_term = jnp.dot(keys_t, dscores[...], preferred_element_type=F32)
        for j in range(TILES):
            q_acc[h, j] += q_term[:, j * 256:(j + 1) * 256]
        terms[pl.ds(2 * c, 2), h, 0] = (k_term * SCALE).reshape(2, BLOCK, HEAD_DIM)
        terms[pl.ds(2 * c, 2), h, 1] = v_term.reshape(2, BLOCK, HEAD_DIM)
        v_sum[h] += jnp.sum(v_term, axis=0, keepdims=True)

    def rs(d, h, n):
        to, step = SUMS[d]
        return remote(sum_out.at[d, h, n], sum_in.at[to, h, n], rs_send.at[d, h, n], rs_recv.at[to, h, n], (dp, z_peer(step), tp))

    def arrived(into, h, n):
        at = sum_in.at[into, h, n]
        remote(at, at, rs_send.at[into, h, n], rs_recv.at[into, h, n], (dp, z_peer(1), tp)).wait_recv()

    def send_sum(d, h):
        def send(mine, before):
            for n in range(2):
                amount = None
                if before:
                    arrived(d, h, n)
                    amount = sum_in[d, h, n]
                if mine:
                    term = terms[SLOT[d], h, n]
                    amount = (term if amount is None else term + amount.astype(F32)).astype(BF16)
                sum_out[d, h, n] = amount
                rs(d, h, n).start()

        if d in (7, 2, 8):
            pl.when(held(d))(lambda: send(True, False))
        elif d <= 7:
            pl.when((me >= d) & (me < RING - 1))(lambda: send(True, True))
            pl.when(me == RING - 1)(lambda: send(True, False))
        else:
            pl.when(me >= d)(lambda: send(True, True))
            pl.when(held(d) & (me < d))(lambda: send(False, True))

    arrivals = {
        2: [(d, h) for h in range(KV) for d in (3, 12)],
        4: [(1, 0), (1, 1), (4, 0), (11, 0), (4, 1), (11, 1)],
        6: [(2, 0), (2, 1)],
        8: [(5, 0), (10, 0), (5, 1), (10, 1)],
        10: [(6, 0), (9, 0), (6, 1), (9, 1)],
        12: [(7, 0), (8, 0)],
        14: [(7, 1), (8, 1)],
    }
    leaving = {
        13: [(7, 0), (8, 0)],
        15: [(7, 1), (8, 1)],
        17: [(6, 0), (9, 0)],
        20: [(6, 1), (9, 1)],
        23: [(5, 0), (10, 0)],
        25: [(2, 0), (2, 1)],
        26: [(5, 1), (10, 1)],
    }

    def unit(t, _):
        for at, blocks in arrivals.items():
            @pl.when(t == at)
            def _(blocks=blocks):
                for d, h in blocks:
                    pass_on(d, h)

        u = t - t // 14
        c = u // 2

        @pl.when(((t <= 12) | (t == 14)) & (me >= nearest(c)))
        def _():
            forward(c, u % 2)

        @pl.when(t == 1)
        def _():
            for h in range(KV):
                send_own(1, h)

        pl.when(t == 12)(lambda: finish(0))
        pl.when(t == 14)(lambda: finish(1))

        u2 = t - 14 + (27 - t) // 14
        o = u2 // 2
        c2 = 6 - o - (o + 4) // 7 + 3 * ((o + 2) // 7) - 2 * ((o + 1) // 7)

        @pl.when(((t == 13) | (t >= 15)) & (me >= nearest(c2)))
        def _():
            backward(c2, u2 % 2)

        pl.when(t == 19)(write_attention)

        for at, sums in leaving.items():
            @pl.when(t == at)
            def _(sums=sums):
                for d, h in sums:
                    send_sum(d, h)

        return 0

    lax.fori_loop(0, UNITS, unit, 0)

    rows = share.shape[1]

    def put(row, sums):
        share[row // rows, row % rows] = sums

    lane = lax.broadcasted_iota(jnp.int32, (8, 2 * BLOCK), 1) // BLOCK
    pick = (lane == lax.broadcasted_iota(jnp.int32, (8, 2 * BLOCK), 0)).astype(F32) * SCALE
    for h in range(KV):
        for j in range(TILES):
            both = lax.dot_general(
                pick, q_acc[h, j], (((1,), (1,)), ((), ())), precision=lax.Precision.HIGHEST, preferred_element_type=F32
            )
            for e in range(2):
                put(2 * (h * GROUP + j * 2 + e), both[e:e + 1])
        put(2 * h + 1, v_sum[h])

    def ar_d(o):
        return remote(share.at[d_peer(o)], share_d.at[o], ar_send.at[0, o], ar_recv.at[0, o], (d_peer(o), me, tp))

    def ar_z(o):
        return remote(part, share_z.at[o], ar_send.at[1, o], ar_recv.at[1, o], (dp, z_peer(o), tp))

    def ar_back(o):
        return remote(sums.at[dp], sums.at[dp], ar_send.at[2, o], ar_recv.at[2, o], (d_peer(o), me, tp))

    def ar_back_in(o):
        source = lax.rem(dp + dps - o, dps)
        return remote(sums.at[source], sums.at[source], ar_send.at[2, o], ar_recv.at[2, o], (d_peer(o), me, tp))

    def each(last, act):
        def body(o, _):
            act(o)
            return 0

        lax.fori_loop(1, last, body, 0)

    def farthest_first(act):
        def body(i, _):
            act(RING // 2 + ((i + 1) // 2) * (1 - 2 * ((i + 1) % 2)))
            return 0

        lax.fori_loop(0, RING - 1, body, 0)

    each(dps, lambda o: ar_d(o).start())
    for h in range(KV):
        for j in range(TILES):
            for e in range(2):
                at = (h * GROUP + j * 2 + e) * 128
                qg_out[:, at:at + 128] = (q_acc[h, j, :, e * 128:(e + 1) * 128] * SCALE).astype(BF16).T
        send_sum(4, h)
        send_sum(11, h)
    stores[1].start()
    for h in range(KV):
        send_sum(1, h)
    each(dps, lambda o: ar_d(o).wait_recv())
    share_d[0] = share[dp]
    part[...] = jnp.sum(share_d[...], axis=0)
    farthest_first(lambda o: ar_z(o).start())
    for h in range(KV):
        send_sum(3, h)
        send_sum(12, h)
    each(RING, lambda o: ar_z(o).wait_recv())
    share_z[0] = part[...]
    sums[dp] = jnp.sum(share_z[...], axis=0) * (1.0 / dps)
    each(dps, lambda o: ar_back(o).start())

    for h in range(KV):
        for d, into in ((1, 0), (3, 2), (12, 7)):
            @pl.when(me <= 7 if d == 12 else me + d < RING)
            def _(into=into, h=h):
                for n in range(2):
                    arrived(into, h, n)
                    terms[0, h, n] = terms[0, h, n] + sum_in[into, h, n].astype(F32)
        kg_ref[:, h * 128:(h + 1) * 128] = terms[0, h, 0].astype(BF16)
        vg_ref[:, h * 128:(h + 1) * 128] = terms[0, h, 1].astype(BF16)

    stores[2].start()
    stores[3].start()

    for to in FIRST:
        @pl.when(me <= 7 if to == 12 else me + to < RING)
        def _(to=to):
            for h in range(KV):
                for n in range(2):
                    ag(0, to, h, n).wait_send()
    for d, to in NEXT.items():
        @pl.when(sends(d, to))
        def _(d=d, to=to):
            for h in range(KV):
                for n in range(2):
                    ag(d, to, h, n).wait_send()
    for d in SUMS:
        @pl.when(held(d))
        def _(d=d):
            for h in range(KV):
                for n in range(2):
                    rs(d, h, n).wait_send()
    each(dps, lambda o: ar_d(o).wait_send())

    each(dps, lambda o: ar_back_in(o).wait_recv())
    for row in range(2 * KV * GROUP):
        if row % 2 == 0:
            qbg_ref[row // 2:row // 2 + 1, :] = sums[row // rows, row % rows]
        elif row < 2 * KV:
            vbg_ref[row // 2:row // 2 + 1, :] = sums[row // rows, row % rows]
    stores[4].start()
    stores[5].start()
    each(RING, lambda o: ar_z(o).wait_send())
    each(dps, lambda o: ar_back(o).wait_send())
    for copy in stores:
        copy.wait()


def write_out(*refs):
    count = 6
    sources, results, held = refs[:count], refs[count:2 * count], refs[2 * count:3 * count]
    sem_in, sem_out = refs[3 * count:]
    parts = []
    for i in range(count):
        rows = sources[i].shape[0]
        step = 32 if rows == BLOCK else rows
        parts += [(i, pl.ds(at, step)) for at in range(0, rows, step)]
    ins = [pltpu.make_async_copy(sources[i].at[at], held[i].at[at], sem_in.at[n]) for n, (i, at) in enumerate(parts)]
    outs = [pltpu.make_async_copy(held[i].at[at], results[i].at[at], sem_out.at[n]) for n, (i, at) in enumerate(parts)]
    for copy in ins:
        copy.start()
    for copy, onward in zip(ins, outs):
        copy.wait()
        onward.start()
    for copy in outs:
        copy.wait()


def shards(q_proj, q_bias, k_proj, v_proj, v_bias, dout, lengths):
    width, kv_width = q_proj.shape[2], k_proj.shape[2]
    dps = lax.axis_size("dp")
    hbm = pl.BlockSpec(memory_space=pltpu.HBM)
    block = (KV, 2, BLOCK, HEAD_DIM)
    results = (
        jax.ShapeDtypeStruct((BLOCK, width), BF16),
        jax.ShapeDtypeStruct((BLOCK, width), BF16),
        jax.ShapeDtypeStruct((BLOCK, kv_width), BF16),
        jax.ShapeDtypeStruct((BLOCK, kv_width), BF16),
        jax.ShapeDtypeStruct((KV * GROUP, HEAD_DIM), F32),
        jax.ShapeDtypeStruct((KV, HEAD_DIM), F32),
    )
    held = pl.pallas_call(
        kernel,
        out_shape=results,
        in_specs=[hbm] * 7,
        out_specs=(hbm,) * 6,
        scratch_shapes=[
            *(pltpu.VMEM(result.shape, result.dtype) for result in results),
            pltpu.VMEM((BLOCK, width), BF16),
            pltpu.VMEM((KV * GROUP, HEAD_DIM), BF16),
            pltpu.VMEM((BLOCK, kv_width), BF16),
            pltpu.VMEM((BLOCK, kv_width), BF16),
            pltpu.VMEM((KV, HEAD_DIM), BF16),
            pltpu.VMEM((BLOCK, width), BF16),
            pltpu.SMEM(lengths.shape, jnp.int32),
            pltpu.VMEM((KV, TILES, 2 * BLOCK, HEAD_DIM), BF16),
            pltpu.VMEM((KV, TILES, 2 * BLOCK, HEAD_DIM), BF16),
            pltpu.VMEM((KV, TILES, HEAD_DIM, 2 * BLOCK), BF16),
            pltpu.VMEM((KV, TILES, HEAD_DIM, 2 * BLOCK), BF16),
            pltpu.VMEM((2 * CHUNKS,) + block, BF16),
            pltpu.VMEM((CHUNKS, KV, TILES, 2 * BLOCK, 2 * BLOCK), F32),
            pltpu.VMEM((KV, TILES, 1, 2 * BLOCK), F32),
            pltpu.VMEM((KV, TILES, 1, 2 * BLOCK), F32),
            pltpu.VMEM((KV, TILES, 1, 2 * BLOCK), F32),
            pltpu.VMEM((KV, TILES, HEAD_DIM, 2 * BLOCK), F32),
            pltpu.VMEM((KV, TILES, HEAD_DIM, 2 * BLOCK), F32),
            pltpu.VMEM((2 * CHUNKS,) + block, F32),
            pltpu.VMEM((KV, TILES, HEAD_DIM, 2 * BLOCK), BF16),
            pltpu.VMEM((2 * BLOCK, GROUP * BLOCK), BF16),
            pltpu.VMEM((2 * BLOCK, GROUP * BLOCK), BF16),
            pltpu.VMEM((KV, 1, HEAD_DIM), F32),
            pltpu.VMEM((13,) + block, BF16),
            pltpu.VMEM((13,) + block, BF16),
            pltpu.VMEM((dps, ROWS // dps, 1, HEAD_DIM), F32),
            pltpu.VMEM((dps, ROWS // dps, 1, HEAD_DIM), F32),
            pltpu.VMEM((ROWS // dps, 1, HEAD_DIM), F32),
            pltpu.VMEM((RING, ROWS // dps, 1, HEAD_DIM), F32),
            pltpu.VMEM((dps, ROWS // dps, 1, HEAD_DIM), F32),
            pltpu.SemaphoreType.DMA((7,)),
            pltpu.SemaphoreType.DMA((6,)),
            pltpu.SemaphoreType.DMA((13, KV, 2)),
            pltpu.SemaphoreType.DMA((13, KV, 2)),
            pltpu.SemaphoreType.DMA((13, KV, 2)),
            pltpu.SemaphoreType.DMA((13, KV, 2)),
            pltpu.SemaphoreType.DMA((3, RING)),
            pltpu.SemaphoreType.DMA((3, RING)),
        ],
        compiler_params=pltpu.CompilerParams(
            collective_id=0, has_side_effects=True, vmem_limit_bytes=60 * 2**20
        ),
        cost_estimate=pl.CostEstimate(flops=6 * 10**9, bytes_accessed=3 * 10**6, transcendentals=7 * 10**6),
        name="attention",
    )(
        q_proj[0],
        q_bias.reshape(-1, HEAD_DIM),
        k_proj[0],
        v_proj[0],
        v_bias.reshape(-1, HEAD_DIM),
        dout[0],
        lengths,
    )
    attn, q_grad, k_grad, v_grad, q_sums, v_sums = pl.pallas_call(
        write_out,
        out_shape=results,
        in_specs=[hbm] * 6,
        out_specs=(hbm,) * 6,
        scratch_shapes=[
            *(pltpu.VMEM(result.shape, result.dtype) for result in results),
            pltpu.SemaphoreType.DMA((18,)),
            pltpu.SemaphoreType.DMA((18,)),
        ],
        compiler_params=pltpu.CompilerParams(vmem_limit_bytes=60 * 2**20),
        name="write_out",
    )(*held)
    return attn[None], q_grad[None], k_grad[None], v_grad[None], q_sums.reshape(-1), v_sums.reshape(-1)


def solution(mesh):
    placed = (
        P("dp", "ctx", "tp"),
        P("tp"),
        P("dp", "ctx", "tp"),
        P("dp", "ctx", "tp"),
        P("tp"),
        P("dp", "ctx", "tp"),
        P("dp", None),
    )
    return jax.shard_map(
        shards,
        mesh=mesh,
        in_specs=placed,
        out_specs=(
            P("dp", "ctx", "tp"),
            P("dp", "ctx", "tp"),
            P("dp", "ctx", "tp"),
            P("dp", "ctx", "tp"),
            P("tp"),
            P("tp"),
        ),
        check_vma=False,
    )
```

```python
import math

import jax
import jax.numpy as jnp
from jax import lax
from jax.experimental import pallas as pl
from jax.experimental.pallas import tpu as pltpu
from jax.sharding import PartitionSpec as P

HEAD_DIM = 128
SCALE = HEAD_DIM ** -0.5
LOG2E = math.log2(math.e)
NEG = -1e30
BLOCK = 128
KV = 2
GROUP = 8
TILES = 4
RING = 16
CHUNKS = 7
F32 = jnp.float32
BF16 = jnp.bfloat16

PAIRS = ((0, None), (3, 12), (4, 11), (1, 2), (5, 10), (6, 9), (7, 8))
SLOT = {d: 2 * c + n for c, pair in enumerate(PAIRS) for n, d in enumerate(pair) if d is not None}
NEXT = {1: 2, 3: 4, 4: 5, 5: 6, 6: 7, 12: 11, 11: 10, 10: 9, 9: 8}
FIRST = (12, 3, 1)
UNITS = 2 * CHUNKS * KV
SUMS = {7: (6, -1), 6: (5, -1), 5: (4, -1), 4: (3, -1), 3: (2, -3), 2: (1, -1), 1: (0, -1),
        8: (9, 1), 9: (10, 1), 10: (11, 1), 11: (12, 1), 12: (7, 4)}
STEPS = (1, -1, 3, -3, 4, -4)
ROWS = 2 * KV * GROUP


def nearest(c):
    return (c + 2) * ((c + 6) // 7) - 4 * ((c + 4) // 7) + 3 * ((c + 3) // 7)


def kernel(
    q_hbm, qb_hbm, k_hbm, v_hbm, vb_hbm, g_hbm, len_hbm,
    attn_hbm, qg_hbm, kg_hbm, vg_hbm, qbg_hbm, vbg_hbm,
    attn_out, qg_out, kg_ref, vg_ref, qbg_ref, vbg_ref, q_in, qb_in, k_in, v_in, vb_in, g_in, lens, q_rows, g_rows, q_cols, g_cols, kv, scores, top, total, delta, acc, q_acc, terms, attn_t, probs_b, dscores,
    v_sum, sum_in, sum_out, share, share_d, part, share_z, sums,
    load_sem, store_sem, ag_send, ag_recv, rs_send, rs_recv, ar_send, ar_recv,
):
    dp, me, tp = lax.axis_index("dp"), lax.axis_index("ctx"), lax.axis_index("tp")
    dps = lax.axis_size("dp")

    def z_peer(o):
        return lax.rem(me + RING + o, RING)

    def d_peer(o):
        return lax.rem(dp + o, dps)

    loads = [
        pltpu.make_async_copy(src, dst, load_sem.at[i])
        for i, (src, dst) in enumerate((
            (k_hbm, k_in), (v_hbm, v_in), (vb_hbm, vb_in), (q_hbm, q_in), (g_hbm, g_in), (qb_hbm, qb_in), (len_hbm, lens)))
    ]
    for copy in loads[:3]:
        copy.start()

    stores = [
        pltpu.make_async_copy(src, dst, store_sem.at[i])
        for i, (src, dst) in enumerate((
            (attn_out, attn_hbm), (qg_out, qg_hbm), (kg_ref, kg_hbm), (vg_ref, vg_hbm), (qbg_ref, qbg_hbm), (vbg_ref, vbg_hbm)))
    ]
    barrier = pltpu.get_barrier_semaphore()

    for step in STEPS:
        pl.semaphore_signal(barrier, inc=1, device_id=(dp, z_peer(step), tp), device_id_type=pl.DeviceIdType.MESH)

    def greet_d(o, _):
        pl.semaphore_signal(barrier, inc=1, device_id=(d_peer(o), me, tp), device_id_type=pl.DeviceIdType.MESH)
        return 0

    lax.fori_loop(1, dps, greet_d, 0)
    for copy in loads[3:]:
        copy.start()

    def remote(src, dst, send, recv, device):
        return pltpu.make_async_remote_copy(
            src_ref=src, dst_ref=dst, send_sem=send, recv_sem=recv, device_id=device, device_id_type=pl.DeviceIdType.MESH
        )

    def held(d):
        return me >= d if d <= 7 else lax.rem(me + RING - d, RING) <= 7

    def ag(d, to, h, n):
        step = to - d if to <= 7 else (-4 if d == 0 else -1)
        return remote(kv.at[SLOT[d], h, n], kv.at[SLOT[to], h, n], ag_send.at[to, h, n], ag_recv.at[to, h, n], (dp, z_peer(step), tp))

    def sends(d, to):
        return (held(d) & (me + to - d < RING)) if to <= 7 else held(d)

    for copy in loads[:3]:
        copy.wait()
    for h in range(KV):
        cols = slice(h * 128, (h + 1) * 128)
        kv[0, h, 0] = k_in[:, cols]
        kv[0, h, 1] = (v_in[:, cols].astype(F32) + vb_in[h:h + 1, :].astype(F32)).astype(BF16)
    nothing = jnp.zeros((KV, 2, BLOCK, HEAD_DIM), BF16)
    pl.semaphore_wait(barrier, len(STEPS) + dps - 1)

    def send_own(to, h):
        @pl.when(me <= 7 if to == 12 else me + to < RING)
        def _():
            for n in range(2):
                ag(0, to, h, n).start()

    for h in range(KV):
        send_own(12, h)
        send_own(3, h)

    for d in (2, 8, 9, 10, 11, 12):
        @pl.when(jnp.logical_not(held(d)))
        def _(d=d):
            kv[SLOT[d]] = nothing

    for copy in loads[3:]:
        copy.wait()
    for h in range(KV):
        for j in range(TILES):
            for e in range(2):
                head = h * GROUP + j * 2 + e
                cols = slice(head * 128, (head + 1) * 128)
                rows = slice(e * 128, (e + 1) * 128)
                block = (q_in[:, cols].astype(F32) + qb_in[head:head + 1, :].astype(F32)).astype(BF16)
                q_rows[h, j, rows, :] = block
                q_cols[h, j, :, rows] = block.T
                block = g_in[:, cols]
                g_rows[h, j, rows, :] = block
                g_cols[h, j, :, rows] = block.T
    top[...] = jnp.full(top.shape, NEG, F32)
    total[...] = jnp.zeros(total.shape, F32)
    acc[...] = jnp.zeros(acc.shape, F32)
    q_acc[...] = jnp.zeros(q_acc.shape, F32)
    v_sum[...] = jnp.zeros(v_sum.shape, F32)
    share[...] = jnp.zeros(share.shape, F32)

    position = me * BLOCK + lax.broadcasted_iota(jnp.int32, (1, BLOCK), 1)
    begin = jnp.zeros((1, BLOCK), jnp.int32)
    end = jnp.int32(0)
    for d in range(lens.shape[1]):
        end = end + lens[0, d]
        begin = jnp.where(position >= end, end, begin)

    def forward(c, h, count):
        near = nearest(c)
        far = jnp.where(c == 0, -1, jnp.where(c == 3, 2, jnp.where(c <= 2, 13 - c, 14 - c)))
        offset = lax.broadcasted_iota(jnp.int32, (BLOCK, BLOCK), 0)
        bias = []
        for d in (near, far)[:count]:
            at = (me - d) * BLOCK + offset
            bias.append(jnp.where((at >= begin) & (at <= position), 0.0, NEG).astype(F32))
        bias = jnp.concatenate(bias, axis=0)
        size = count * BLOCK
        pair = kv[pl.ds(2 * c, count), h]
        keys = pair[:, 0].reshape(size, HEAD_DIM)
        values_t = pair[:, 1].reshape(size, HEAD_DIM).T
        for j in range(TILES):
            for e in range(2):
                at = slice(e * 128, (e + 1) * 128)
                score = jnp.dot(keys, q_cols[h, j, :, at], preferred_element_type=F32) * (SCALE * LOG2E) + bias
                scores[c, h, j, :size, at] = score
                old = top[h, j, :, at]
                new = jnp.maximum(old, jnp.max(score, axis=0, keepdims=True))
                fade = jnp.exp2(old - new)
                weights = jnp.exp2(score - new)
                top[h, j, :, at] = new
                total[h, j, :, at] = total[h, j, :, at] * fade + jnp.sum(weights, axis=0, keepdims=True)
                acc[h, j, :, at] = acc[h, j, :, at] * fade + jnp.dot(
                    values_t, weights.astype(BF16), preferred_element_type=F32)

    def pass_on(d, h):
        @pl.when(held(d))
        def _():
            for n in range(2):
                ag(d, d, h, n).wait_recv()
                if d in NEXT:
                    to = NEXT[d]
                    if to <= 7:
                        @pl.when(me + 1 < RING)
                        def _():
                            ag(d, to, h, n).start()
                    else:
                        ag(d, to, h, n).start()

    def finish(h):
        for j in range(TILES):
            amount = total[h, j]
            out = (acc[h, j] * (1.0 / amount)).astype(BF16)
            delta[h, j] = jnp.sum(out.astype(F32) * g_cols[h, j].astype(F32), axis=0, keepdims=True)
            top[h, j] = top[h, j] + jnp.log2(amount)
            attn_t[h, j] = out

    def write_attention():
        for h in range(KV):
            for j in range(TILES):
                for e in range(2):
                    at = (h * GROUP + j * 2 + e) * 128
                    attn_out[:, at:at + 128] = attn_t[h, j, :, e * 128:(e + 1) * 128].T
        stores[0].start()

    def backward(c, h, count):
        size = count * BLOCK
        pair = kv[pl.ds(2 * c, count), h]
        keys_t = pair[:, 0].reshape(size, HEAD_DIM).T
        values = pair[:, 1].reshape(size, HEAD_DIM)
        for j in range(TILES):
            at = slice(j * 256, (j + 1) * 256)
            probs = jnp.exp2(scores[c, h, j, :size] - top[h, j])
            dprob = jnp.dot(values, g_cols[h, j], preferred_element_type=F32)
            dscores[:size, at] = (probs * (dprob - delta[h, j])).astype(BF16)
            probs_b[:size, at] = probs.astype(BF16)
        v_term = jnp.dot(probs_b[:size], g_rows[h].reshape(GROUP * BLOCK, HEAD_DIM), preferred_element_type=F32)
        k_term = jnp.dot(dscores[:size], q_rows[h].reshape(GROUP * BLOCK, HEAD_DIM), preferred_element_type=F32)
        q_term = jnp.dot(keys_t, dscores[:size], preferred_element_type=F32)
        for j in range(TILES):
            q_acc[h, j] += q_term[:, j * 256:(j + 1) * 256]
        terms[pl.ds(2 * c, count), h, 0] = (k_term * SCALE).reshape(count, BLOCK, HEAD_DIM)
        terms[pl.ds(2 * c, count), h, 1] = v_term.reshape(count, BLOCK, HEAD_DIM)
        v_sum[h] += jnp.sum(v_term, axis=0, keepdims=True)

    def rs(d, h, n):
        to, step = SUMS[d]
        return remote(sum_out.at[d, h, n], sum_in.at[to, h, n], rs_send.at[d, h, n], rs_recv.at[to, h, n], (dp, z_peer(step), tp))

    def arrived(into, h, n):
        at = sum_in.at[into, h, n]
        remote(at, at, rs_send.at[into, h, n], rs_recv.at[into, h, n], (dp, z_peer(1), tp)).wait_recv()

    def send_sum(d, h):
        def send(mine, before):
            for n in range(2):
                amount = None
                if before:
                    arrived(d, h, n)
                    amount = sum_in[d, h, n]
                if mine:
                    term = terms[SLOT[d], h, n]
                    amount = (term if amount is None else term + amount.astype(F32)).astype(BF16)
                sum_out[d, h, n] = amount
                rs(d, h, n).start()

        if d in (7, 2, 8):
            pl.when(held(d))(lambda: send(True, False))
        elif d <= 7:
            pl.when((me >= d) & (me < RING - 1))(lambda: send(True, True))
            pl.when(me == RING - 1)(lambda: send(True, False))
        else:
            pl.when(me >= d)(lambda: send(True, True))
            pl.when(held(d) & (me < d))(lambda: send(False, True))

    arrivals = {
        2: [(d, h) for h in range(KV) for d in (3, 12)],
        4: [(1, 0), (1, 1), (4, 0), (11, 0), (4, 1), (11, 1)],
        6: [(2, 0), (2, 1)],
        8: [(5, 0), (10, 0), (5, 1), (10, 1)],
        10: [(6, 0), (9, 0), (6, 1), (9, 1)],
        12: [(7, 0), (8, 0)],
        14: [(7, 1), (8, 1)],
    }
    leaving = {
        13: [(7, 0), (8, 0)],
        15: [(7, 1), (8, 1)],
        17: [(6, 0), (9, 0)],
        20: [(6, 1), (9, 1)],
        23: [(5, 0), (10, 0)],
        25: [(2, 0), (2, 1)],
        26: [(5, 1), (10, 1)],
    }

    def unit(t, _):
        for at, blocks in arrivals.items():
            @pl.when(t == at)
            def _(blocks=blocks):
                for d, h in blocks:
                    pass_on(d, h)

        u = t - t // 14
        c = u // 2

        @pl.when(t < 2)
        def _():
            forward(0, t, 1)

        @pl.when((((t >= 2) & (t <= 12)) | (t == 14)) & (me >= nearest(c)))
        def _():
            forward(c, u % 2, 2)

        @pl.when(t == 1)
        def _():
            for h in range(KV):
                send_own(1, h)

        pl.when(t == 12)(lambda: finish(0))
        pl.when(t == 14)(lambda: finish(1))

        u2 = t - 14 + (27 - t) // 14
        o = u2 // 2
        c2 = 6 - o - (o + 4) // 7 + 3 * ((o + 2) // 7) - 2 * ((o + 1) // 7)

        @pl.when(((t == 13) | (t >= 15)) & (t < 26) & (me >= nearest(c2)))
        def _():
            backward(c2, u2 % 2, 2)

        @pl.when(t >= 26)
        def _():
            backward(0, u2 % 2, 1)

        for at, sums in leaving.items():
            @pl.when(t == at)
            def _(sums=sums):
                for d, h in sums:
                    send_sum(d, h)

        return 0

    lax.fori_loop(0, UNITS, unit, 0)

    rows = share.shape[1]

    def put(row, sums):
        share[row // rows, row % rows] = sums

    lane = lax.broadcasted_iota(jnp.int32, (8, 2 * BLOCK), 1) // BLOCK
    pick = (lane == lax.broadcasted_iota(jnp.int32, (8, 2 * BLOCK), 0)).astype(F32) * SCALE
    for h in range(KV):
        for j in range(TILES):
            both = lax.dot_general(
                pick, q_acc[h, j], (((1,), (1,)), ((), ())), precision=lax.Precision.HIGHEST, preferred_element_type=F32
            )
            for e in range(2):
                put(2 * (h * GROUP + j * 2 + e), both[e:e + 1])
        put(2 * h + 1, v_sum[h])

    def ar_d(o):
        return remote(share.at[d_peer(o)], share_d.at[o], ar_send.at[0, o], ar_recv.at[0, o], (d_peer(o), me, tp))

    def ar_z(o):
        return remote(part, share_z.at[o], ar_send.at[1, o], ar_recv.at[1, o], (dp, z_peer(o), tp))

    def ar_back(o):
        return remote(sums.at[dp], sums.at[dp], ar_send.at[2, o], ar_recv.at[2, o], (d_peer(o), me, tp))

    def ar_back_in(o):
        source = lax.rem(dp + dps - o, dps)
        return remote(sums.at[source], sums.at[source], ar_send.at[2, o], ar_recv.at[2, o], (d_peer(o), me, tp))

    def each(last, act):
        def body(o, _):
            act(o)
            return 0

        lax.fori_loop(1, last, body, 0)

    def farthest_first(act):
        def body(i, _):
            act(RING // 2 + ((i + 1) // 2) * (1 - 2 * ((i + 1) % 2)))
            return 0

        lax.fori_loop(0, RING - 1, body, 0)

    each(dps, lambda o: ar_d(o).start())
    for d in (4, 11, 1):
        for h in range(KV):
            send_sum(d, h)
    each(dps, lambda o: ar_d(o).wait_recv())
    share_d[0] = share[dp]
    part[...] = jnp.sum(share_d[...], axis=0)
    farthest_first(lambda o: ar_z(o).start())
    for h in range(KV):
        send_sum(3, h)
        send_sum(12, h)

    write_attention()
    for h in range(KV):
        for j in range(TILES):
            for e in range(2):
                at = (h * GROUP + j * 2 + e) * 128
                qg_out[:, at:at + 128] = (q_acc[h, j, :, e * 128:(e + 1) * 128] * SCALE).astype(BF16).T
    stores[1].start()
    each(RING, lambda o: ar_z(o).wait_recv())
    share_z[0] = part[...]
    sums[dp] = jnp.sum(share_z[...], axis=0) * (1.0 / dps)
    each(dps, lambda o: ar_back(o).start())

    for h in range(KV):
        for d, into in ((1, 0), (3, 2), (12, 7)):
            @pl.when(me <= 7 if d == 12 else me + d < RING)
            def _(into=into, h=h):
                for n in range(2):
                    arrived(into, h, n)
                    terms[0, h, n] = terms[0, h, n] + sum_in[into, h, n].astype(F32)
        kg_ref[:, h * 128:(h + 1) * 128] = terms[0, h, 0].astype(BF16)
        vg_ref[:, h * 128:(h + 1) * 128] = terms[0, h, 1].astype(BF16)

    stores[2].start()
    stores[3].start()

    for to in FIRST:
        @pl.when(me <= 7 if to == 12 else me + to < RING)
        def _(to=to):
            for h in range(KV):
                for n in range(2):
                    ag(0, to, h, n).wait_send()
    for d, to in NEXT.items():
        @pl.when(sends(d, to))
        def _(d=d, to=to):
            for h in range(KV):
                for n in range(2):
                    ag(d, to, h, n).wait_send()
    for d in SUMS:
        @pl.when(held(d))
        def _(d=d):
            for h in range(KV):
                for n in range(2):
                    rs(d, h, n).wait_send()
    each(dps, lambda o: ar_d(o).wait_send())

    each(dps, lambda o: ar_back_in(o).wait_recv())
    for row in range(2 * KV * GROUP):
        if row % 2 == 0:
            qbg_ref[row // 2:row // 2 + 1, :] = sums[row // rows, row % rows]
        elif row < 2 * KV:
            vbg_ref[row // 2:row // 2 + 1, :] = sums[row // rows, row % rows]
    stores[4].start()
    stores[5].start()
    each(RING, lambda o: ar_z(o).wait_send())
    each(dps, lambda o: ar_back(o).wait_send())
    for copy in stores:
        copy.wait()


def write_out(*refs):
    count = 6
    sources, results, held = refs[:count], refs[count:2 * count], refs[2 * count:3 * count]
    sem_in, sem_out = refs[3 * count:]
    parts = []
    for i in range(count):
        rows = sources[i].shape[0]
        step = 32 if rows == BLOCK else rows
        parts += [(i, pl.ds(at, step)) for at in range(0, rows, step)]
    ins = [pltpu.make_async_copy(sources[i].at[at], held[i].at[at], sem_in.at[n]) for n, (i, at) in enumerate(parts)]
    outs = [pltpu.make_async_copy(held[i].at[at], results[i].at[at], sem_out.at[n]) for n, (i, at) in enumerate(parts)]
    for copy in ins:
        copy.start()
    for copy, onward in zip(ins, outs):
        copy.wait()
        onward.start()
    for copy in outs:
        copy.wait()


def shards(q_proj, q_bias, k_proj, v_proj, v_bias, dout, lengths):
    width, kv_width = q_proj.shape[2], k_proj.shape[2]
    dps = lax.axis_size("dp")
    hbm = pl.BlockSpec(memory_space=pltpu.HBM)
    block = (KV, 2, BLOCK, HEAD_DIM)
    results = (
        jax.ShapeDtypeStruct((BLOCK, width), BF16),
        jax.ShapeDtypeStruct((BLOCK, width), BF16),
        jax.ShapeDtypeStruct((BLOCK, kv_width), BF16),
        jax.ShapeDtypeStruct((BLOCK, kv_width), BF16),
        jax.ShapeDtypeStruct((KV * GROUP, HEAD_DIM), F32),
        jax.ShapeDtypeStruct((KV, HEAD_DIM), F32),
    )
    held = pl.pallas_call(
        kernel,
        out_shape=results,
        in_specs=[hbm] * 7,
        out_specs=(hbm,) * 6,
        scratch_shapes=[
            *(pltpu.VMEM(result.shape, result.dtype) for result in results),
            pltpu.VMEM((BLOCK, width), BF16),
            pltpu.VMEM((KV * GROUP, HEAD_DIM), BF16),
            pltpu.VMEM((BLOCK, kv_width), BF16),
            pltpu.VMEM((BLOCK, kv_width), BF16),
            pltpu.VMEM((KV, HEAD_DIM), BF16),
            pltpu.VMEM((BLOCK, width), BF16),
            pltpu.SMEM(lengths.shape, jnp.int32),
            pltpu.VMEM((KV, TILES, 2 * BLOCK, HEAD_DIM), BF16),
            pltpu.VMEM((KV, TILES, 2 * BLOCK, HEAD_DIM), BF16),
            pltpu.VMEM((KV, TILES, HEAD_DIM, 2 * BLOCK), BF16),
            pltpu.VMEM((KV, TILES, HEAD_DIM, 2 * BLOCK), BF16),
            pltpu.VMEM((2 * CHUNKS,) + block, BF16),
            pltpu.VMEM((CHUNKS, KV, TILES, 2 * BLOCK, 2 * BLOCK), F32),
            pltpu.VMEM((KV, TILES, 1, 2 * BLOCK), F32),
            pltpu.VMEM((KV, TILES, 1, 2 * BLOCK), F32),
            pltpu.VMEM((KV, TILES, 1, 2 * BLOCK), F32),
            pltpu.VMEM((KV, TILES, HEAD_DIM, 2 * BLOCK), F32),
            pltpu.VMEM((KV, TILES, HEAD_DIM, 2 * BLOCK), F32),
            pltpu.VMEM((2 * CHUNKS,) + block, F32),
            pltpu.VMEM((KV, TILES, HEAD_DIM, 2 * BLOCK), BF16),
            pltpu.VMEM((2 * BLOCK, GROUP * BLOCK), BF16),
            pltpu.VMEM((2 * BLOCK, GROUP * BLOCK), BF16),
            pltpu.VMEM((KV, 1, HEAD_DIM), F32),
            pltpu.VMEM((13,) + block, BF16),
            pltpu.VMEM((13,) + block, BF16),
            pltpu.VMEM((dps, ROWS // dps, 1, HEAD_DIM), F32),
            pltpu.VMEM((dps, ROWS // dps, 1, HEAD_DIM), F32),
            pltpu.VMEM((ROWS // dps, 1, HEAD_DIM), F32),
            pltpu.VMEM((RING, ROWS // dps, 1, HEAD_DIM), F32),
            pltpu.VMEM((dps, ROWS // dps, 1, HEAD_DIM), F32),
            pltpu.SemaphoreType.DMA((7,)),
            pltpu.SemaphoreType.DMA((6,)),
            pltpu.SemaphoreType.DMA((13, KV, 2)),
            pltpu.SemaphoreType.DMA((13, KV, 2)),
            pltpu.SemaphoreType.DMA((13, KV, 2)),
            pltpu.SemaphoreType.DMA((13, KV, 2)),
            pltpu.SemaphoreType.DMA((3, RING)),
            pltpu.SemaphoreType.DMA((3, RING)),
        ],
        compiler_params=pltpu.CompilerParams(
            collective_id=0, has_side_effects=True, vmem_limit_bytes=60 * 2**20
        ),
        cost_estimate=pl.CostEstimate(flops=6 * 10**9, bytes_accessed=3 * 10**6, transcendentals=7 * 10**6),
        name="attention",
    )(
        q_proj[0],
        q_bias.reshape(-1, HEAD_DIM),
        k_proj[0],
        v_proj[0],
        v_bias.reshape(-1, HEAD_DIM),
        dout[0],
        lengths,
    )
    attn, q_grad, k_grad, v_grad, q_sums, v_sums = pl.pallas_call(
        write_out,
        out_shape=results,
        in_specs=[hbm] * 6,
        out_specs=(hbm,) * 6,
        scratch_shapes=[
            *(pltpu.VMEM(result.shape, result.dtype) for result in results),
            pltpu.SemaphoreType.DMA((18,)),
            pltpu.SemaphoreType.DMA((18,)),
        ],
        compiler_params=pltpu.CompilerParams(vmem_limit_bytes=60 * 2**20),
        name="write_out",
    )(*held)
    return attn[None], q_grad[None], k_grad[None], v_grad[None], q_sums.reshape(-1), v_sums.reshape(-1)


def solution(mesh):
    placed = (
        P("dp", "ctx", "tp"),
        P("tp"),
        P("dp", "ctx", "tp"),
        P("dp", "ctx", "tp"),
        P("tp"),
        P("dp", "ctx", "tp"),
        P("dp", None),
    )
    return jax.shard_map(
        shards,
        mesh=mesh,
        in_specs=placed,
        out_specs=(
            P("dp", "ctx", "tp"),
            P("dp", "ctx", "tp"),
            P("dp", "ctx", "tp"),
            P("dp", "ctx", "tp"),
            P("tp"),
            P("tp"),
        ),
        check_vma=False,
    )
```
